32 devices in a mesh: ctx: 8 (over z, y), fsdp: 4 (over x, core).
Axes of the slice: x: 2, y: 2, z: 4, core: 2. Of those that a mesh axis runs over, the one named last changes fastest.
Arguments:
- tokens: bfloat16 [4, 3584, 1024], P('fsdp', 'ctx'), may hold values from -6 to 6
- cotangent: bfloat16 [4, 3584, 1024], P('fsdp', 'ctx'), may hold values from -6 to 6
- block_table: int32 [16], replicated, may hold values from 0 to 15, as said below
- mixer_gain: float32 [1024], replicated, may hold values from 0.5 to 1.5
- in_proj: bfloat16 [1024, 3352], P('fsdp'), may hold values from -0.1875 to 0.1875
- conv_weight: float32 [4, 1792], replicated, may hold values from -0.5 to 0.5
- conv_bias: float32 [1792], replicated, may hold values from -0.5 to 0.5
- step_bias: float32 [24], replicated, may hold values from -3 to 0
- decay_log: float32 [24], replicated, may hold values from -20 to 0, as said below
- skip_gain: float32 [24], replicated, may hold values from 0.5 to 1.5
- gated_gain: float32 [1536], replicated, may hold values from 0.5 to 1.5
- out_proj: bfloat16 [1536, 1024], P('fsdp'), may hold values from -0.15625 to 0.15625
- attention_in: bfloat16 [1024, 768], P('fsdp'), may hold values from -0.1875 to 0.1875
- attention_out: bfloat16 [512, 1024], P('fsdp'), may hold values from -6 to 6
- feed_gain: float32 [1024], replicated, may hold values from 0.5 to 1.5
- gate_up: bfloat16 [1024, 4096], P('fsdp'), may hold values from -0.1875 to 0.1875
- down_proj: bfloat16 [2048, 1024], P('fsdp'), may hold values from -0.125 to 0.125
Outputs:
- output: bfloat16 [4, 3584, 1024], P('fsdp', 'ctx')
- input_grad: float32 [4, 3584, 1024], P('fsdp', 'ctx')
- grad_mixer_gain: float32 [1024], replicated
- grad_in_proj: float32 [1024, 3352], P(('ctx', 'fsdp'))
- grad_conv_weight: float32 [4, 1792], replicated
- grad_conv_bias: float32 [1792], replicated
- grad_step_bias: float32 [24], replicated
- grad_decay_log: float32 [24], replicated
- grad_skip_gain: float32 [24], replicated
- grad_gated_gain: float32 [1536], replicated
- grad_out_proj: float32 [1536, 1024], P(('ctx', 'fsdp'))
- grad_attention_in: float32 [1024, 768], P(('ctx', 'fsdp'))
- grad_attention_out: float32 [512, 1024], P(('ctx', 'fsdp'))
- grad_feed_gain: float32 [1024], replicated
- grad_gate_up: float32 [1024, 4096], P(('ctx', 'fsdp'))
- grad_down_proj: float32 [2048, 1024], P(('ctx', 'fsdp'))
The draws below stay inside these ranges and needn't reach their ends.
Inputs may be any that keep to these rules, and one draw needn't show every extreme that they name: `block_table`: entries 2 d and 2 d + 1 hold the blocks d and 15 - d, in an order drawn for each d. exp(decay_log) lies between 0.2 / 224 and 4 / 224.
All inputs are finite; a program needn't handle non-finite values.
Results may differ from the reference program's by a relative error of at most 0.014.
The reference program's roundings to bfloat16 on the way count: a program that leaves them out, or rounds other values in their place, can miss the bound.
Values may be sent and summed in bfloat16 or wider, within the bound.
No kernel may reach another device: no remote copies, remote signals or barrier semaphores. Data moves between devices by JAX's collectives and lax.ppermute only.
A program may use at most 256 MiB of HBM per device.

```python
import jax
import jax.numpy as jnp
from jax import lax

D = 1024
DI = 1536
MH = 24
MP = 64
NS = 128
KCONV = 4
QUERY_HEADS = 8
KEY_VALUE_HEADS = 2
HEAD_WIDTH = 64
FF = 2048
HB = 224
SEQUENCE_TOKENS = 3584
NBLK = 16
SEQS = 4
CONV = 1792
IN_COLS = 3352
QKV = 768


def draw_block_table(key, part):
    key = jax.random.fold_in(key, 7)
    flips_drawn = jax.random.randint(key, (NBLK // 2,), 0, 2)
    early_blocks = jnp.arange(NBLK // 2, dtype=jnp.int32)
    late_blocks = NBLK - 1 - early_blocks
    first_slot = jnp.where(flips_drawn == 1, late_blocks, early_blocks)
    second_slot = jnp.where(flips_drawn == 1, early_blocks, late_blocks)
    return jnp.stack([first_slot, second_slot], axis=1).reshape(NBLK).astype(jnp.int32)


def draw_decay_log(key, part):
    key = jax.random.fold_in(key, 11)
    lowest = jnp.log(jnp.float32(0.2) / HB)
    highest_rate = jnp.log(jnp.float32(4.0) / HB)
    fraction = jax.random.uniform(key, (MH,), jnp.float32)
    return (lowest + fraction * (highest_rate - lowest)).astype(jnp.float32)


def shard_levels(rng, dims, cuts, low, top_value):
    def one(position, parts):
        heights = jax.random.uniform(jax.random.fold_in(jax.random.fold_in(rng, 6), position), (parts,), jnp.float32, low / len(cuts), top_value / len(cuts))
        return jnp.repeat(jnp.exp(heights), dims[position] // parts).reshape((-1,) + (1,) * (len(dims) - position - 1))

    factor_of = one(*cuts[0])
    for cut in cuts[1:]:
        factor_of = factor_of * one(*cut)
    return factor_of


def scatter_about(rng, dims, width, limit, cuts=(), held_as=jnp.bfloat16):
    loudness = shard_levels(rng, dims, cuts, -0.22, 0.18) if cuts else 1.0
    array = jax.random.normal(rng, dims, jnp.float32) * width * loudness
    return jnp.minimum(jnp.maximum(array, -limit), limit).astype(held_as)


def setup_inputs(seed: int = 0) -> dict:
    seeds = jax.random.split(jax.random.key(seed), 18)
    return {
        "tokens": scatter_about(seeds[0], (SEQS, SEQUENCE_TOKENS, D), 1.0, 6.0, ((0, 4), (1, 8))),
        "cotangent": scatter_about(seeds[1], (SEQS, SEQUENCE_TOKENS, D), 1.0, 6.0, ((0, 4), (1, 8))),
        "block_table": draw_block_table(jax.random.fold_in(seeds[17], 71), 0),
        "mixer_gain": jnp.clip(1.0 + 0.1 * jax.random.normal(seeds[3], (D,), jnp.float32), 0.5, 1.5),
        "in_proj": scatter_about(seeds[4], (D, IN_COLS), D ** -0.5, 0.1875, ((0, 4),)),
        "conv_weight": jnp.clip(jax.random.uniform(seeds[5], (KCONV, CONV), jnp.float32, -0.5, 0.5), -0.5, 0.5),
        "conv_bias": jnp.clip(jax.random.uniform(seeds[6], (CONV,), jnp.float32, -0.5, 0.5), -0.5, 0.5),
        "step_bias": jnp.clip(jax.random.uniform(seeds[7], (MH,), jnp.float32, -3.0, 0.0), -3.0, 0.0),
        "decay_log": draw_decay_log(jax.random.fold_in(seeds[17], 71), 0),
        "skip_gain": jnp.clip(jax.random.uniform(seeds[9], (MH,), jnp.float32, 0.5, 1.5), 0.5, 1.5),
        "gated_gain": jnp.clip(1.0 + 0.1 * jax.random.normal(seeds[10], (DI,), jnp.float32), 0.5, 1.5),
        "out_proj": scatter_about(seeds[11], (DI, D), DI ** -0.5, 0.15625, ((0, 4),)),
        "attention_in": scatter_about(seeds[12], (D, QKV), D ** -0.5, 0.1875, ((0, 4),)),
        "attention_out": scatter_about(seeds[13], (QUERY_HEADS * HEAD_WIDTH, D), (SEQUENCE_TOKENS // 4096 + 1), 6.0, ((0, 4),)),
        "feed_gain": jnp.clip(1.0 + 0.1 * jax.random.normal(seeds[14], (D,), jnp.float32), 0.5, 1.5),
        "gate_up": scatter_about(seeds[15], (D, 2 * FF), D ** -0.5, 0.1875, ((0, 4),)),
        "down_proj": scatter_about(seeds[16], (FF, D), FF ** -0.5, 0.125, ((0, 4),)),
    }


highest = lax.Precision.HIGHEST
epsilon = 1e-05
rope_base = 100000000000.0
score_scale = 0.125
masked_fill_value = -1e+30

@jax.custom_vjp
def low(v):
    return lax.optimization_barrier(v.astype(jnp.bfloat16)).astype(jnp.float32)

@jax.custom_vjp
def low_back(v):
    return v

def low_keep(v):
    return (low(v), None)

def low_pass(kept, grad):
    return (grad,)

def back_keep(v):
    return (v, None)

def back_low(kept, grad):
    return (low(grad),)
low.defvjp(low_keep, low_pass)
low_back.defvjp(back_keep, back_low)

def norm_scale(value_rows):
    return lax.rsqrt(lax.optimization_barrier(jnp.mean(value_rows * value_rows, axis=-1, keepdims=True)) + epsilon)

def matmul(left, right):
    return jnp.dot(left, right, precision=highest, preferred_element_type=jnp.float32)

def rotary_embedding(value_rows, token_positions, direction):
    half_size = value_rows.shape[-1] // 2
    freqs = jnp.exp(-(jnp.arange(half_size, dtype=jnp.float32) * (2.0 / value_rows.shape[-1])) * jnp.log(rope_base))
    angles = token_positions.astype(jnp.float32)[:, None] * freqs[None, :]
    cosine = jnp.cos(angles)[:, None, :]
    sine = direction * jnp.sin(angles)[:, None, :]
    first_half = value_rows[..., :half_size]
    second_half = value_rows[..., half_size:]
    return jnp.concatenate([first_half * cosine - second_half * sine, second_half * cosine + first_half * sine], axis=-1)

def conv_block(previous, raw_rows, conv_weight, conv_bias):
    extended = jnp.concatenate([previous, raw_rows], axis=0)
    row_count = raw_rows.shape[0]
    running = conv_bias[None, :] + conv_weight[0][None, :] * extended[0:row_count]
    for offset in range(1, conv_weight.shape[0]):
        running = running + conv_weight[offset][None, :] * extended[offset:offset + row_count]
    return jax.nn.silu(running)

def scan_local(inputs, b_rows, c_rows, step_size, decay_rate, skip_gain):
    log_decay = step_size * decay_rate[None, :]
    cumulative = jnp.cumsum(log_decay, axis=0)
    row_count = inputs.shape[0]
    causal = jnp.arange(row_count)[:, None] >= jnp.arange(row_count)[None, :]
    log_gap = cumulative.T[:, :, None] - cumulative.T[:, None, :]
    decays = jnp.exp(jnp.where(causal[None], log_gap, masked_fill_value))
    pair_scores = jnp.dot(c_rows, b_rows.T, precision=highest)
    weighted = decays * pair_scores[None]
    scaled_in = inputs * step_size[:, :, None]
    partial_out = jnp.einsum('hts,shp->thp', weighted, scaled_in, precision=highest) + skip_gain[None, :, None] * inputs
    tail_decay = jnp.exp(cumulative[-1][None, :] - cumulative)
    update = jnp.einsum('sh,shp,sn->hpn', tail_decay, scaled_in, b_rows, precision=highest)
    return (partial_out, cumulative, update)

def scan_carry(state_in, c_rows, cumulative):
    return jnp.einsum('hpn,tn->thp', state_in, c_rows, precision=highest) * jnp.exp(cumulative)[:, :, None]

def scan_block(inputs, b_rows, c_rows, step_size, decay_rate, skip_gain, state_in):
    partial_out, cumulative, update = scan_local(inputs, b_rows, c_rows, step_size, decay_rate, skip_gain)
    result = partial_out + scan_carry(state_in, c_rows, cumulative)
    state_out = jnp.exp(cumulative[-1])[:, None, None] * state_in + update
    return (result, state_out)

def layer(hidden, mixer_gain, in_proj, conv_weight, conv_bias, step_bias, decay_log, skip_gain, gated_gain, out_proj, attention_in, attention_out, feed_gain, gate_up, down_proj):
    normed_one = low(hidden * norm_scale(hidden) * mixer_gain)
    projected = low_back(matmul(normed_one, in_proj))
    query_key_value_rows = low_back(matmul(normed_one, attention_in))
    gate_z = projected[:, :DI]
    raw_conv = projected[:, DI:DI + CONV]
    step_raw = projected[:, DI + CONV:]
    mixed = conv_block(jnp.zeros((KCONV - 1, CONV), jnp.float32), raw_conv, conv_weight, conv_bias)
    inputs = mixed[:, :DI].reshape(SEQUENCE_TOKENS, MH, MP)
    b_rows = mixed[:, DI:DI + NS]
    c_rows = mixed[:, DI + NS:]
    step_size = jax.nn.softplus(step_raw + step_bias[None, :])
    decay_rate = -jnp.exp(decay_log)

    def span_step(state, pieces):
        result, state_next = scan_block(pieces[0], pieces[1], pieces[2], pieces[3], decay_rate, skip_gain, state)
        return (state_next, result)
    start_state = jnp.zeros((MH, MP, NS), jnp.float32)
    _, span_outs = lax.scan(jax.checkpoint(span_step), start_state, (inputs.reshape(NBLK, HB, MH, MP), b_rows.reshape(NBLK, HB, NS), c_rows.reshape(NBLK, HB, NS), step_size.reshape(NBLK, HB, MH)))
    scan_out = span_outs.reshape(SEQUENCE_TOKENS, DI)
    gated = scan_out * jax.nn.silu(gate_z)
    gated_low = low(gated * norm_scale(gated) * gated_gain)
    mamba_out = low_back(matmul(gated_low, out_proj))
    token_positions = jnp.arange(SEQUENCE_TOKENS, dtype=jnp.int32)
    query_matrix = low(rotary_embedding(query_key_value_rows[:, :QUERY_HEADS * HEAD_WIDTH].reshape(SEQUENCE_TOKENS, QUERY_HEADS, HEAD_WIDTH), token_positions, 1.0))
    key_rows = low(rotary_embedding(query_key_value_rows[:, QUERY_HEADS * HEAD_WIDTH:(QUERY_HEADS + KEY_VALUE_HEADS) * HEAD_WIDTH].reshape(SEQUENCE_TOKENS, KEY_VALUE_HEADS, HEAD_WIDTH), token_positions, 1.0))
    value_rows = low(query_key_value_rows[:, (QUERY_HEADS + KEY_VALUE_HEADS) * HEAD_WIDTH:].reshape(SEQUENCE_TOKENS, KEY_VALUE_HEADS, HEAD_WIDTH))
    query_row_slice = min(512, SEQUENCE_TOKENS)
    grouped_heads = query_matrix.reshape(SEQUENCE_TOKENS // query_row_slice, query_row_slice, KEY_VALUE_HEADS, QUERY_HEADS // KEY_VALUE_HEADS, HEAD_WIDTH)

    def attend(pieces):
        block_q, start = pieces
        scores = low_back(jnp.einsum('qgrd,kgd->grqk', block_q, key_rows, precision=highest) * score_scale)
        query_pos = start + jnp.arange(query_row_slice, dtype=jnp.int32)
        allowed = token_positions[None, :] <= query_pos[:, None]
        scores = jnp.where(allowed[None, None], scores, masked_fill_value)
        probs = low(jax.nn.softmax(scores, axis=-1))
        return low_back(jnp.einsum('grqk,kgd->qgrd', probs, value_rows, precision=highest))
    starts = jnp.arange(SEQUENCE_TOKENS // query_row_slice, dtype=jnp.int32) * query_row_slice
    attended = lax.map(jax.checkpoint(attend), (grouped_heads, starts)).reshape(SEQUENCE_TOKENS, QUERY_HEADS * HEAD_WIDTH)
    attn_out = low_back(matmul(low(attended), attention_out))
    second = hidden + mamba_out + attn_out
    normed_two = low(second * norm_scale(second) * feed_gain)
    gate_rows = low_back(matmul(normed_two, gate_up))
    activated = low(jax.nn.silu(gate_rows[:, :FF]) * gate_rows[:, FF:])
    down_rows = low_back(matmul(activated, down_proj))
    return second + down_rows

def reference(tokens, cotangent, block_table, mixer_gain, in_proj, conv_weight, conv_bias, step_bias, decay_log, skip_gain, gated_gain, out_proj, attention_in, attention_out, feed_gain, gate_up, down_proj):
    slot_of = jnp.argsort(block_table).astype(jnp.int32)

    def arrange(value_rows):
        return value_rows.reshape(SEQS, NBLK, HB, D)[:, slot_of].reshape(SEQS, SEQUENCE_TOKENS, D)

    def restore(value_rows):
        return value_rows.reshape(SEQS, NBLK, HB, D)[:, block_table].reshape(SEQS, SEQUENCE_TOKENS, D)
    hidden = arrange(tokens.astype(jnp.float32))
    weights = tuple((tensor.astype(jnp.float32) for tensor in (mixer_gain, in_proj, conv_weight, conv_bias, step_bias, decay_log, skip_gain, gated_gain, out_proj, attention_in, attention_out, feed_gain, gate_up, down_proj)))

    def whole(hidden_all, weight_set):
        return lax.map(lambda sequence: layer(sequence, *weight_set), hidden_all)
    output, pullback = jax.vjp(whole, hidden, weights)
    hidden_grad, weight_grads = pullback(arrange(cotangent.astype(jnp.float32)))
    return (restore(output).astype(jnp.bfloat16), restore(hidden_grad), weight_grads[0], weight_grads[1], weight_grads[2], weight_grads[3], weight_grads[4], weight_grads[5], weight_grads[6], weight_grads[7], weight_grads[8], weight_grads[9], weight_grads[10], weight_grads[11], weight_grads[12], weight_grads[13])
```

```python
import math

import jax
import jax.numpy as jnp
from jax import lax
from jax.experimental import pallas as pl
from jax.experimental.pallas import tpu as pltpu
from jax.sharding import PartitionSpec as P

DI = 1536
MH = 24
MP = 64
NS = 128
KCONV = 4
QUERY_HEADS = 8
KEY_VALUE_HEADS = 2
HEAD_WIDTH = 64
GROUP = QUERY_HEADS // KEY_VALUE_HEADS
FF = 2048
CONV = 1792
PAIRS = MH // 2

highest = lax.Precision.HIGHEST
epsilon = 1e-05
rope_base = 100000000000.0
score_scale = 0.125
masked_fill_value = -1e30
bf16 = jnp.bfloat16
f32 = jnp.float32


def xor_pairs(count, distance):
    return [(i, i ^ distance) for i in range(count)]


def swap(array, axis, distance):
    return lax.ppermute(array, axis, xor_pairs(lax.axis_size(axis), distance))


def norm_scale(value_rows):
    return lax.rsqrt(jnp.mean(value_rows * value_rows, axis=-1, keepdims=True) + epsilon)


def norm_backward(grad_norm, value_rows, scale):
    return scale * (
        grad_norm
        - value_rows * scale * scale * jnp.mean(grad_norm * value_rows, axis=-1, keepdims=True)
    )


def matmul(left, right):
    return jnp.dot(left, right, preferred_element_type=f32)


def row_contract(left, right):
    return lax.dot_general(left, right, (((0,), (0,)), ((), ())), preferred_element_type=f32)


def backward_product(grad_rows, weight):
    return lax.dot_general(grad_rows, weight, (((1,), (1,)), ((), ())), preferred_element_type=f32)


def edge_exchange(array, width):
    devices, length = lax.axis_size("ctx"), array.shape[0]
    up = [(i, i + 1) for i in range(devices - 1)]
    down = [(j, i) for i, j in up]
    before = lax.ppermute(array[length - width :], "ctx", up)
    after = lax.ppermute(array[:width], "ctx", down)
    return before, after


def gather_weight_fast(weight):
    fs = lax.axis_index("fsdp")
    rows, cols = weight.shape
    half = rows // 2
    y_bit, x_bit, c_bit = lax.axis_index("ctx") % 2, fs // 2, fs % 2
    mine = lax.dynamic_slice_in_dim(weight, y_bit * half, half, 0)
    first = swap(mine, "fsdp", 2)
    second = swap(first, "ctx", 1)
    buf = jnp.zeros((2, 2, 2, half, cols), weight.dtype)
    zero = jnp.int32(0)

    def put(buf, piece, x, c, h):
        piece = piece.reshape(1, 1, -1, half, cols)
        return lax.dynamic_update_slice(buf, piece, (x, c, h, zero, zero))

    buf = put(buf, weight, x_bit, c_bit, zero)
    buf = put(buf, swap(weight, "fsdp", 1), x_bit, 1 - c_bit, zero)
    buf = put(buf, first, 1 - x_bit, c_bit, y_bit)
    buf = put(buf, swap(first, "fsdp", 1), 1 - x_bit, 1 - c_bit, y_bit)
    buf = put(buf, second, 1 - x_bit, c_bit, 1 - y_bit)
    buf = put(buf, swap(second, "fsdp", 1), 1 - x_bit, 1 - c_bit, 1 - y_bit)
    return buf.reshape(4 * rows, cols)


def gather_weight(weight, fast):
    if fast and lax.axis_size("fsdp") == 4 and lax.axis_size("ctx") % 2 == 0:
        return gather_weight_fast(weight)
    return lax.all_gather(weight, "fsdp", axis=0, tiled=True)


def gather_ctx(piece):
    count = lax.axis_size("ctx")
    outer = jnp.stack([piece] + [swap(piece, "ctx", k) for k in range(2, count, 2)])
    both = jnp.stack([outer, swap(outer, "ctx", 1)], axis=1)
    return both.reshape((count,) + piece.shape)


def reduce_ctx(stacked):
    count = lax.axis_size("ctx")
    parts = stacked.reshape((count // 2, 2) + stacked.shape[1:])
    parts = (parts[:, 0].astype(f32) + swap(parts[:, 1], "ctx", 1).astype(f32)).astype(bf16)
    total = parts[0].astype(f32)
    for k in range(2, count, 2):
        total = total + swap(parts[k // 2], "ctx", k).astype(f32)
    return total


def pick(array, index, dim):
    return lax.dynamic_index_in_dim(array, index, dim, keepdims=False)


def exchange_sum(array, dim, axis, stride, size):
    own = (lax.axis_index(axis) // stride) % size
    total = pick(array, own, dim).astype(f32)
    for k in range(1, size):
        total = total + swap(pick(array, own ^ k, dim), axis, k * stride).astype(f32)
    return total


def rows_by_owner(grad):
    ctx_count, fs_count = lax.axis_size("ctx"), lax.axis_size("fsdp")
    rows, cols = grad.shape
    return grad.astype(bf16).reshape(
        ctx_count // 2, 2, fs_count // 2, 2, rows // (ctx_count * fs_count), cols
    )


def sum_core(views):
    core = lax.axis_index("fsdp") % 2
    keep, send = (
        jnp.concatenate([pick(view, side, 3) for view in views], axis=3) for side in (core, 1 - core)
    )
    return (keep.astype(f32) + swap(send, "fsdp", 1).astype(f32)).astype(bf16)


def sum_first(parts):
    half, wide = parts.shape[0] // 2, parts.shape[2]
    low = exchange_sum(parts[:half], 2, "fsdp", 2, wide).astype(bf16)
    high = exchange_sum(parts[half:], 1, "ctx", 1, 2).astype(bf16)
    return low, high


def sum_second(low, high):
    low = exchange_sum(low, 1, "ctx", 1, 2).astype(bf16)
    high = exchange_sum(high, 1, "fsdp", 2, high.shape[1]).astype(bf16)
    return jnp.concatenate([low, high], axis=0)


def sum_last(parts):
    return exchange_sum(parts, 0, "ctx", 2, parts.shape[0])


def tie(*arrays):
    return lax.optimization_barrier(arrays)


def all_sum(array):
    for axis in ("fsdp", "ctx"):
        distance = 1
        while distance < lax.axis_size(axis):
            array = array + swap(array, axis, distance)
            distance *= 2
    return array


def pair_table(ctx_count, mine):
    step = jnp.arange(2 * ctx_count + 1, dtype=jnp.int32)
    late = step > mine
    key_block = jnp.where(late, step - (mine + 1), step)
    own = jnp.where(late, 2 * ctx_count - 1 - mine, mine)
    key_late = key_block >= ctx_count
    device = jnp.where(key_late, 2 * ctx_count - 1 - key_block, key_block)
    place = (device ^ mine) * 2 + key_late.astype(jnp.int32)
    return jnp.stack(
        [
            late.astype(jnp.int32),
            place,
            (key_block == 0).astype(jnp.int32),
            (key_block == own).astype(jnp.int32),
        ]
    )


def turn(x, cosine, sine):
    lane = lax.broadcasted_iota(jnp.int32, x.shape, 1) % HEAD_WIDTH
    swapped = jnp.where(
        lane < HEAD_WIDTH // 2,
        pltpu.roll(x, 2 * HEAD_WIDTH - HEAD_WIDTH // 2, 1),
        pltpu.roll(x, HEAD_WIDTH // 2, 1),
    )
    return x * cosine + swapped * sine


def side_by_side(rows):
    turned = [rows[:, 2 * HEAD_WIDTH * p : 2 * HEAD_WIDTH * (p + 1)].T for p in range(QUERY_HEADS // 2)]
    heads = [turned[h // 2][h % 2 * HEAD_WIDTH : (h % 2 + 1) * HEAD_WIDTH] for h in range(QUERY_HEADS)]
    return [
        jnp.concatenate(heads[g * GROUP : (g + 1) * GROUP], axis=1).astype(bf16)
        for g in range(KEY_VALUE_HEADS)
    ]


def head_pair(groups, pair):
    half = groups[0].shape[1] // GROUP
    heads = []
    for h in (2 * pair, 2 * pair + 1):
        k = h % GROUP
        heads.append(groups[h // GROUP][:, k * half : (k + 1) * half])
    return jnp.concatenate(heads, axis=0).T


def prepare_kernel(qkv_ref, cos_ref, sin_ref, q_ref, pair_ref):
    width = 2 * HEAD_WIDTH
    cosine, sine = cos_ref[...], sin_ref[...]
    queries = []
    for p in range(QUERY_HEADS // 2):
        turned = turn(qkv_ref[:, width * p : width * (p + 1)], cosine, sine)
        queries.append(turned.astype(bf16).astype(f32) * score_scale)
    for g, part in enumerate(side_by_side(jnp.concatenate(queries, axis=1))):
        q_ref[0, g] = part
    start = QUERY_HEADS * HEAD_WIDTH
    pair_ref[:, :width] = turn(qkv_ref[:, start : start + width], cosine, sine).astype(bf16)
    pair_ref[:, width:] = qkv_ref[:, start + width :].astype(bf16)


def prepare(qkv_rows, cosine, sine):
    half = qkv_rows.shape[0] // 2
    kv = KEY_VALUE_HEADS * HEAD_WIDTH
    turn_spec = pl.BlockSpec((half, 2 * HEAD_WIDTH), lambda b: (b, 0))
    return pl.pallas_call(
        prepare_kernel,
        grid=(2,),
        in_specs=[pl.BlockSpec((half, qkv_rows.shape[1]), lambda b: (b, 0)), turn_spec, turn_spec],
        out_specs=[
            pl.BlockSpec((1, KEY_VALUE_HEADS, HEAD_WIDTH, GROUP * half), lambda b: (b, 0, 0, 0)),
            pl.BlockSpec((half, 2 * kv), lambda b: (b, 0)),
        ],
        out_shape=[
            jax.ShapeDtypeStruct((2, KEY_VALUE_HEADS, HEAD_WIDTH, GROUP * half), bf16),
            jax.ShapeDtypeStruct((2 * half, 2 * kv), bf16),
        ],
        compiler_params=pltpu.CompilerParams(vmem_limit_bytes=24 * 2**20),
        cost_estimate=pl.CostEstimate(flops=2**22, bytes_accessed=2**22, transcendentals=0),
        name="prepare",
    )(qkv_rows, cosine, sine)


def attn_forward_kernel(tab, q_ref, kv_ref, row_ref, o_ref, ot_ref, lse_ref, m_s, l_s, acc_s):
    step = pl.program_id(0)
    diag = tab[3, step]

    @pl.when(tab[2, step] == 1)
    def _():
        m_s[...] = jnp.full(m_s.shape, masked_fill_value, f32)
        l_s[...] = jnp.zeros(l_s.shape, f32)
        acc_s[...] = jnp.zeros(acc_s.shape, f32)

    keys, queries = kv_ref.shape[1], q_ref.shape[3]
    limit = row_ref[...] + (1 - diag) * keys
    allowed = lax.broadcasted_iota(jnp.int32, (keys, queries), 0) <= limit
    kv = kv_ref[0]
    values_t = kv[:, KEY_VALUE_HEADS * HEAD_WIDTH :].astype(f32).T.astype(bf16)
    for g in range(KEY_VALUE_HEADS):
        head = slice(g * HEAD_WIDTH, (g + 1) * HEAD_WIDTH)
        scores = matmul(kv[:, head], q_ref[0, g])
        scores = jnp.where(allowed, scores, masked_fill_value)
        old = m_s[g]
        new = jnp.maximum(old, jnp.max(scores, axis=0, keepdims=True))
        probs = jnp.exp(scores - new)
        fade = jnp.exp(old - new)
        m_s[g] = new
        l_s[g] = l_s[g] * fade + jnp.sum(probs, axis=0, keepdims=True)
        acc_s[g] = acc_s[g] * fade + matmul(values_t[head], probs.astype(bf16))

    @pl.when(diag == 1)
    def _():
        outs = []
        for g in range(KEY_VALUE_HEADS):
            outs.append(acc_s[g] / l_s[g])
            ot_ref[0, g] = outs[g]
            lse_ref[0, g] = m_s[g] + jnp.log(l_s[g])
        for p in range(QUERY_HEADS // 2):
            o_ref[:, 2 * HEAD_WIDTH * p : 2 * HEAD_WIDTH * (p + 1)] = head_pair(outs, p).astype(bf16)


def attn_specs(half):
    width = GROUP * half
    query = pl.BlockSpec((1, KEY_VALUE_HEADS, HEAD_WIDTH, width), lambda j, t: (t[0, j], 0, 0, 0))
    row = pl.BlockSpec((1, KEY_VALUE_HEADS, 1, width), lambda j, t: (t[0, j], 0, 0, 0))
    pair = pl.BlockSpec((1, half, 2 * KEY_VALUE_HEADS * HEAD_WIDTH), lambda j, t: (t[1, j], 0, 0))
    natural = pl.BlockSpec((half, QUERY_HEADS * HEAD_WIDTH), lambda j, t: (t[0, j], 0))
    return query, row, pair, natural


def attn_forward(table, q_t, all_pairs, query_row):
    steps = table.shape[1]
    half, width = all_pairs.shape[1], q_t.shape[3]
    query, row, pair, natural = attn_specs(half)
    return pl.pallas_call(
        attn_forward_kernel,
        grid_spec=pltpu.PrefetchScalarGridSpec(
            num_scalar_prefetch=1,
            grid=(steps,),
            in_specs=[query, pair, pl.BlockSpec((1, width), lambda j, t: (0, 0))],
            out_specs=[natural, query, row],
            scratch_shapes=[
                pltpu.VMEM((KEY_VALUE_HEADS, 1, width), f32),
                pltpu.VMEM((KEY_VALUE_HEADS, 1, width), f32),
                pltpu.VMEM((KEY_VALUE_HEADS, HEAD_WIDTH, width), f32),
            ],
        ),
        out_shape=[
            jax.ShapeDtypeStruct((2 * half, QUERY_HEADS * HEAD_WIDTH), bf16),
            jax.ShapeDtypeStruct(q_t.shape, f32),
            jax.ShapeDtypeStruct((2, KEY_VALUE_HEADS, 1, width), f32),
        ],
        compiler_params=pltpu.CompilerParams(vmem_limit_bytes=40 * 2**20),
        cost_estimate=pl.CostEstimate(
            flops=steps * 4 * half * width * 2 * HEAD_WIDTH,
            bytes_accessed=2**23,
            transcendentals=steps * 2 * half * width,
        ),
        name="attn_forward",
    )(table, q_t, all_pairs, query_row)


def attn_backward_kernel(
    tab, q_ref, kv_ref, do_ref, ot_ref, lse_ref, cos_ref, sin_ref, row_ref,
    dq_ref, dkv_ref, do_s, dot_s, dq_s, dkv_s,
):
    step = pl.program_id(0)
    diag = tab[3, step]
    place = tab[1, step]

    @pl.when(step == 0)
    def _():
        dkv_s[...] = jnp.zeros(dkv_s.shape, f32)

    @pl.when(tab[2, step] == 1)
    def _():
        dq_s[...] = jnp.zeros(dq_s.shape, f32)
        for g, part in enumerate(side_by_side(do_ref[...].astype(f32))):
            do_s[g] = part
            dot_s[g] = jnp.sum(part.astype(f32) * ot_ref[0, g], axis=0, keepdims=True)

    keys, queries = kv_ref.shape[1], q_ref.shape[3]
    limit = row_ref[...] + (1 - diag) * keys
    allowed = lax.broadcasted_iota(jnp.int32, (keys, queries), 0) <= limit
    kv = kv_ref[0]
    kv_width = KEY_VALUE_HEADS * HEAD_WIDTH
    keys_t = kv[:, :kv_width].astype(f32).T.astype(bf16)
    grads = [None] * 4
    for g in range(KEY_VALUE_HEADS):
        head = slice(g * HEAD_WIDTH, (g + 1) * HEAD_WIDTH)
        v_head = slice(kv_width + g * HEAD_WIDTH, kv_width + (g + 1) * HEAD_WIDTH)
        q, d_out = q_ref[0, g], do_s[g]
        scores = matmul(kv[:, head], q)
        probs = jnp.exp(jnp.where(allowed, scores - lse_ref[0, g], masked_fill_value))
        d_probs = matmul(kv[:, v_head], d_out)
        d_scores = (probs * (d_probs - dot_s[g])).astype(bf16)
        dq_s[g] += matmul(keys_t[head], d_scores)
        grads[g] = backward_product(d_scores, q)
        grads[2 + g] = backward_product(probs.astype(bf16), d_out)
    dkv_s[place] += jnp.concatenate(grads, axis=1)

    @pl.when(diag == 1)
    def _():
        parts = [dq_s[g] for g in range(KEY_VALUE_HEADS)]
        for p in range(QUERY_HEADS // 2):
            turned = turn(head_pair(parts, p), cos_ref[...], -sin_ref[...]) * score_scale
            dq_ref[:, 2 * HEAD_WIDTH * p : 2 * HEAD_WIDTH * (p + 1)] = turned.astype(bf16)

    @pl.when(step == pl.num_programs(0) - 1)
    def _():
        dkv_ref[...] = dkv_s[...].astype(bf16)


def attn_backward(table, q_t, all_pairs, d_out, out_t, lse, cosine, sine, query_row):
    steps = table.shape[1]
    blocks, half, kv = all_pairs.shape
    width = q_t.shape[3]
    query, row, pair, natural = attn_specs(half)
    turn_spec = pl.BlockSpec((half, 2 * HEAD_WIDTH), lambda j, t: (t[0, j], 0))
    return pl.pallas_call(
        attn_backward_kernel,
        grid_spec=pltpu.PrefetchScalarGridSpec(
            num_scalar_prefetch=1,
            grid=(steps,),
            in_specs=[
                query, pair, natural, query, row, turn_spec, turn_spec,
                pl.BlockSpec((1, width), lambda j, t: (0, 0)),
            ],
            out_specs=[natural, pl.BlockSpec((blocks, half, kv), lambda j, t: (0, 0, 0))],
            scratch_shapes=[
                pltpu.VMEM((KEY_VALUE_HEADS, HEAD_WIDTH, width), bf16),
                pltpu.VMEM((KEY_VALUE_HEADS, 1, width), f32),
                pltpu.VMEM((KEY_VALUE_HEADS, HEAD_WIDTH, width), f32),
                pltpu.VMEM((blocks, half, kv), f32),
            ],
        ),
        out_shape=[
            jax.ShapeDtypeStruct((2 * half, QUERY_HEADS * HEAD_WIDTH), bf16),
            jax.ShapeDtypeStruct((blocks, half, kv), bf16),
        ],
        compiler_params=pltpu.CompilerParams(vmem_limit_bytes=56 * 2**20),
        cost_estimate=pl.CostEstimate(
            flops=steps * 10 * half * width * 2 * HEAD_WIDTH,
            bytes_accessed=2**24,
            transcendentals=steps * 2 * half * width,
        ),
        name="attn_backward",
    )(table, q_t, all_pairs, d_out, out_t, lse, cosine, sine, query_row)


def two_halves(values):
    high = values.astype(bf16)
    return high, (values - high.astype(f32)).astype(bf16)


def wide_product(left, right):
    return backward_product(
        jnp.concatenate([left[0], left[0], left[1]], axis=1),
        jnp.concatenate([right[0], right[1], right[0]], axis=1),
    )


def by_pair(columns, pair, left):
    return jnp.where(left, columns[:, 2 * pair : 2 * pair + 1], columns[:, 2 * pair + 1 : 2 * pair + 2])


def pair_lanes(pair):
    return slice(2 * MP * pair, 2 * MP * (pair + 1))


def scan_forward_kernel(m_ref, dt_ref, cum_ref, cumt_ref, skip_ref, part_ref, upd_ref, tail_s):
    half = m_ref.shape[0]
    left = lax.broadcasted_iota(jnp.int32, (half, 2 * MP), 1) < MP
    causal = lax.broadcasted_iota(jnp.int32, (half, half), 0) >= lax.broadcasted_iota(
        jnp.int32, (half, half), 1
    )
    b_rows = m_ref[:, DI : DI + NS].astype(bf16)
    scores = wide_product(two_halves(m_ref[:, DI + NS :]), two_halves(m_ref[:, DI : DI + NS]))
    dt, cum, cum_t = dt_ref[0], cum_ref[0], cumt_ref[0]
    tail = jnp.exp(cum[half - 1 : half, :] - cum)
    for pair in range(PAIRS):
        lanes = pair_lanes(pair)
        x = m_ref[:, lanes]
        scaled = x * by_pair(dt, pair, left)
        scaled_both = jnp.concatenate(two_halves(scaled), axis=1)
        outs = []
        for h in (2 * pair, 2 * pair + 1):
            gap = cum[:, h : h + 1] - cum_t[h : h + 1, :]
            weights = jnp.exp(jnp.where(causal, gap, masked_fill_value)) * scores
            high, rest = two_halves(weights)
            wide = matmul(high, scaled_both)
            outs.append(wide[:, : 2 * MP] + wide[:, 2 * MP :] + matmul(rest, scaled_both[:, : 2 * MP]))
        part_ref[:, lanes] = jnp.where(left, outs[0], outs[1]) + skip_ref[:, lanes] * x
        tail_s[:, lanes] = (scaled * by_pair(tail, pair, left)).astype(bf16)
    upd_ref[0] = row_contract(b_rows, tail_s[...]).astype(bf16)


def token_specs(half):
    per_block = pl.BlockSpec((1, half, MH), lambda b: (b, 0, 0))
    per_block_t = pl.BlockSpec((1, MH, half), lambda b: (b, 0, 0))
    return per_block, per_block_t


def scan_forward(mixed, dt, cum, cum_t, skip_row):
    half = mixed.shape[0] // 2
    per_block, per_block_t = token_specs(half)
    return pl.pallas_call(
        scan_forward_kernel,
        grid=(2,),
        in_specs=[
            pl.BlockSpec((half, CONV), lambda b: (b, 0)),
            per_block,
            per_block,
            per_block_t,
            pl.BlockSpec((1, DI), lambda b: (0, 0)),
        ],
        out_specs=[
            pl.BlockSpec((half, DI), lambda b: (b, 0)),
            pl.BlockSpec((1, NS, DI), lambda b: (b, 0, 0)),
        ],
        out_shape=[
            jax.ShapeDtypeStruct((2 * half, DI), f32),
            jax.ShapeDtypeStruct((2, NS, DI), bf16),
        ],
        scratch_shapes=[pltpu.VMEM((half, DI), bf16)],
        compiler_params=pltpu.CompilerParams(vmem_limit_bytes=48 * 2**20),
        cost_estimate=pl.CostEstimate(
            flops=2 * half * half * 128 * 2 * MH,
            bytes_accessed=16 * half * DI,
            transcendentals=2 * MH * half * half,
        ),
        name="scan_forward",
    )(mixed, dt, cum, cum_t, skip_row)


def state_kernel(order, upd_ref, fade_ref, out_ref):
    def one(i, state):
        place = order[0, i]
        out_ref[place] = state.astype(bf16)
        return state * fade_ref[pl.ds(order[1, i], 1), :] + upd_ref[place].astype(f32)

    lax.fori_loop(0, upd_ref.shape[0], one, jnp.zeros(upd_ref.shape[1:], f32))


def run_states(order, updates, fades):
    return pl.pallas_call(
        state_kernel,
        grid_spec=pltpu.PrefetchScalarGridSpec(
            num_scalar_prefetch=1,
            grid=(1,),
            in_specs=[
                pl.BlockSpec(updates.shape, lambda j, t: (0, 0, 0)),
                pl.BlockSpec(fades.shape, lambda j, t: (0, 0)),
            ],
            out_specs=pl.BlockSpec(updates.shape, lambda j, t: (0, 0, 0)),
        ),
        out_shape=jax.ShapeDtypeStruct(updates.shape, bf16),
        compiler_params=pltpu.CompilerParams(vmem_limit_bytes=24 * 2**20),
        name="run_states",
    )(order, updates, fades)


def exchange_states(order, updates, fades):
    count = lax.axis_size("ctx")
    share = NS // count
    parts = updates.reshape(2, count, share, DI).swapaxes(0, 1)
    pieces = lax.all_to_all(parts, "ctx", 0, 0).reshape(2 * count, share, DI)
    states = run_states(order, pieces, fades).reshape(count, 2, share, DI)
    back = lax.all_to_all(states, "ctx", 0, 0)
    return back.swapaxes(0, 1).reshape(2, NS, DI)


def gated_forward_kernel(part_ref, c_ref, cum_ref, state_ref, z_ref, gain_ref, y_ref, low_ref, g_s):
    half = part_ref.shape[0]
    left = lax.broadcasted_iota(jnp.int32, (half, 2 * MP), 1) < MP
    c_rows, c_rest = two_halves(c_ref[...])
    carried = matmul(c_rows, state_ref[0]) + matmul(c_rest, state_ref[0])
    decay = jnp.exp(cum_ref[0])
    square = jnp.zeros((half, 2 * MP), f32)
    for pair in range(PAIRS):
        lanes = pair_lanes(pair)
        y = part_ref[:, lanes] + carried[:, lanes] * by_pair(decay, pair, left)
        y_ref[:, lanes] = y
        gated = y * jax.nn.silu(z_ref[:, lanes])
        g_s[:, lanes] = gated
        square += gated * gated
    scale = lax.rsqrt(jnp.sum(square, axis=1, keepdims=True) * (1.0 / DI) + epsilon)
    low_ref[...] = (g_s[...] * scale * gain_ref[...]).astype(bf16)


def gated_forward(part, mixed, cum, states, projected, gain):
    half = part.shape[0] // 2
    per_block, _ = token_specs(half)
    wide = pl.BlockSpec((half, DI), lambda b: (b, 0))
    return pl.pallas_call(
        gated_forward_kernel,
        grid=(2,),
        in_specs=[
            wide,
            pl.BlockSpec((half, NS), lambda b: (b, (DI + NS) // NS)),
            per_block,
            pl.BlockSpec((1, NS, DI), lambda b: (b, 0, 0)),
            wide,
            pl.BlockSpec((1, DI), lambda b: (0, 0)),
        ],
        out_specs=[wide, wide],
        out_shape=[
            jax.ShapeDtypeStruct((2 * half, DI), f32),
            jax.ShapeDtypeStruct((2 * half, DI), bf16),
        ],
        scratch_shapes=[pltpu.VMEM((half, DI), f32)],
        compiler_params=pltpu.CompilerParams(vmem_limit_bytes=48 * 2**20),
        cost_estimate=pl.CostEstimate(
            flops=4 * half * NS * DI + 40 * half * DI,
            bytes_accessed=30 * half * DI,
            transcendentals=4 * half * DI,
        ),
        name="gated_forward",
    )(part, mixed, cum, states, projected, gain)


def gated_backward_kernel(
    gg_ref, y_ref, z_ref, gain_ref, c_ref, cum_ref, yg_ref, zg_ref, gain_g_ref, direct_ref, g_s, w_s
):
    half = gg_ref.shape[0]
    left = lax.broadcasted_iota(jnp.int32, (half, 2 * MP), 1) < MP
    decay = jnp.exp(cum_ref[0])
    square = jnp.zeros((half, 2 * MP), f32)
    cross = jnp.zeros((half, 2 * MP), f32)
    for pair in range(PAIRS):
        lanes = pair_lanes(pair)
        gated = y_ref[:, lanes] * jax.nn.silu(z_ref[:, lanes])
        g_s[:, lanes] = gated
        square += gated * gated
        cross += gg_ref[:, lanes] * gain_ref[:, lanes] * gated
    scale = lax.rsqrt(jnp.sum(square, axis=1, keepdims=True) * (1.0 / DI) + epsilon)
    mean = jnp.sum(cross, axis=1, keepdims=True) * (1.0 / DI)
    pull = scale * scale * scale * mean
    for pair in range(PAIRS):
        lanes = pair_lanes(pair)
        gated, grad, z = g_s[:, lanes], gg_ref[:, lanes], z_ref[:, lanes]
        gain_g_ref[0, :, lanes] = jnp.sum(grad * gated * scale, axis=0, keepdims=True)
        inner = scale * grad * gain_ref[:, lanes] - gated * pull
        sig = jax.nn.sigmoid(z)
        zg_ref[:, lanes] = (inner * y_ref[:, lanes] * sig * (1.0 + z * (1.0 - sig))).astype(bf16)
        grad_y = inner * z * sig
        yg_ref[:, lanes] = grad_y
        w_s[:, lanes] = (grad_y * by_pair(decay, pair, left)).astype(bf16)
    direct_ref[0] = row_contract(c_ref[...].astype(bf16), w_s[...]).astype(bf16)


def gated_backward(gated_grad, scan_out, projected, gain, mixed, cum):
    half = gated_grad.shape[0] // 2
    per_block, _ = token_specs(half)
    wide = pl.BlockSpec((half, DI), lambda b: (b, 0))
    return pl.pallas_call(
        gated_backward_kernel,
        grid=(2,),
        in_specs=[
            wide,
            wide,
            wide,
            pl.BlockSpec((1, DI), lambda b: (0, 0)),
            pl.BlockSpec((half, NS), lambda b: (b, (DI + NS) // NS)),
            per_block,
        ],
        out_specs=[
            wide,
            wide,
            pl.BlockSpec((1, 1, DI), lambda b: (b, 0, 0)),
            pl.BlockSpec((1, NS, DI), lambda b: (b, 0, 0)),
        ],
        out_shape=[
            jax.ShapeDtypeStruct((2 * half, DI), f32),
            jax.ShapeDtypeStruct((2 * half, DI), bf16),
            jax.ShapeDtypeStruct((2, 1, DI), f32),
            jax.ShapeDtypeStruct((2, NS, DI), bf16),
        ],
        scratch_shapes=[pltpu.VMEM((half, DI), f32), pltpu.VMEM((half, DI), bf16)],
        compiler_params=pltpu.CompilerParams(vmem_limit_bytes=48 * 2**20),
        cost_estimate=pl.CostEstimate(
            flops=4 * half * NS * DI + 60 * half * DI,
            bytes_accessed=40 * half * DI,
            transcendentals=8 * half * DI,
        ),
        name="gated_backward",
    )(gated_grad, scan_out, projected, gain, mixed, cum)


def split_sum(values, spread):
    high, rest = two_halves(values)
    return matmul(high, spread) + matmul(rest, spread)


def scan_backward_kernel(
    m_ref, gy_ref, y_ref, dt_ref, cum_ref, cumt_ref, skip_ref, state_ref, carry_ref,
    dm_ref, dcum_ref, ddt_ref, dskip_ref, last_ref, tail_s, grow_s, blt_s,
):
    half = m_ref.shape[0]
    left = lax.broadcasted_iota(jnp.int32, (half, 2 * MP), 1) < MP
    upper = lax.broadcasted_iota(jnp.int32, (half, half), 0) <= lax.broadcasted_iota(
        jnp.int32, (half, half), 1
    )
    b_rows, b_rest = two_halves(m_ref[:, DI : DI + NS])
    c_rows, c_rest = two_halves(m_ref[:, DI + NS :])
    scores_t = wide_product((b_rows, b_rest), (c_rows, c_rest))
    dt, cum, cum_t = dt_ref[0], cum_ref[0], cumt_ref[0]
    grow = jnp.exp(cum)
    tail = jnp.exp(cum[half - 1 : half, :] - cum)
    fade = grow[half - 1 : half, :]
    carry_low = carry_ref[0]
    blt_s[...] = matmul(b_rows, carry_low)
    d_scores_t = jnp.zeros((half, half), f32)
    d_cum = jnp.zeros((half, 2 * MP), f32)
    d_dt = jnp.zeros((half, 2 * MP), f32)
    lane_head = lax.broadcasted_iota(jnp.int32, (2 * MP, 2 * MP), 0) // MP
    column = lax.broadcasted_iota(jnp.int32, (2 * MP, 2 * MP), 1)
    for pair in range(PAIRS):
        lanes = pair_lanes(pair)
        x, gy = m_ref[:, lanes], gy_ref[:, lanes]
        dt_pair = by_pair(dt, pair, left)
        scaled = x * dt_pair
        gy_low, gy_rest = two_halves(gy)
        scaled_two = two_halves(scaled)
        nothing = jnp.zeros_like(gy_low)
        outs = []
        for k, h in enumerate((2 * pair, 2 * pair + 1)):
            gap = cum_t[h : h + 1, :] - cum[:, h : h + 1]
            decays = jnp.exp(jnp.where(upper, gap, masked_fill_value))
            outs.append(matmul((decays * scores_t).astype(bf16), gy_low))
            mine = [jnp.where(left, v, nothing) if k == 0 else jnp.where(left, nothing, v) for v in scaled_two]
            d_scores_t += wide_product(mine, (gy_low, gy_rest)) * decays
        tail_pair = by_pair(tail, pair, left)
        from_tail = tail_pair * blt_s[:, lanes]
        d_scaled = jnp.where(left, outs[0], outs[1]) + from_tail
        dm_ref[:, lanes] = dt_pair * d_scaled + skip_ref[:, lanes] * gy
        spread = (lane_head + 2 * pair == column).astype(bf16)
        skipped = x * gy
        d_cum += split_sum(gy * y_ref[:, lanes] - skip_ref[:, lanes] * skipped - scaled * d_scaled, spread)
        d_dt += split_sum(x * d_scaled, spread)
        dskip_ref[0, :, lanes] = jnp.sum(skipped, axis=0, keepdims=True)
        held = jnp.sum(state_ref[0][:, lanes].astype(f32) * carry_low[:, lanes].astype(f32), axis=0, keepdims=True)
        last_ref[0, :, lanes] = jnp.sum(scaled * from_tail, axis=0, keepdims=True) + held * by_pair(
            fade, pair, left[0:1]
        )
        tail_s[0, :, lanes], tail_s[1, :, lanes] = two_halves(scaled * tail_pair)
        grow_s[0, :, lanes], grow_s[1, :, lanes] = two_halves(gy * by_pair(grow, pair, left))
    d_low, d_rest = two_halves(d_scores_t)
    dm_ref[:, DI : DI + NS] = (
        matmul(d_low, c_rows)
        + matmul(d_low, c_rest)
        + matmul(d_rest, c_rows)
        + backward_product(tail_s[0], carry_low)
        + backward_product(tail_s[1], carry_low)
    )
    dm_ref[:, DI + NS :] = (
        row_contract(d_low, b_rows)
        + row_contract(d_low, b_rest)
        + row_contract(d_rest, b_rows)
        + backward_product(grow_s[0], state_ref[0])
        + backward_product(grow_s[1], state_ref[0])
    )
    dcum_ref[0] = d_cum[:, :MH]
    ddt_ref[0] = d_dt[:, :MH]


def scan_backward(mixed, scan_grad, scan_out, dt, cum, cum_t, skip_row, states, carries):
    half = mixed.shape[0] // 2
    per_block, per_block_t = token_specs(half)
    wide = pl.BlockSpec((half, DI), lambda b: (b, 0))
    full = pl.BlockSpec((half, CONV), lambda b: (b, 0))
    state = pl.BlockSpec((1, NS, DI), lambda b: (b, 0, 0))
    row = pl.BlockSpec((1, 1, DI), lambda b: (b, 0, 0))
    return pl.pallas_call(
        scan_backward_kernel,
        grid=(2,),
        in_specs=[
            full, wide, wide, per_block, per_block, per_block_t,
            pl.BlockSpec((1, DI), lambda b: (0, 0)), state, state,
        ],
        out_specs=[full, per_block, per_block, row, row],
        out_shape=[
            jax.ShapeDtypeStruct((2 * half, CONV), f32),
            jax.ShapeDtypeStruct((2, half, MH), f32),
            jax.ShapeDtypeStruct((2, half, MH), f32),
            jax.ShapeDtypeStruct((2, 1, DI), f32),
            jax.ShapeDtypeStruct((2, 1, DI), f32),
        ],
        scratch_shapes=[
            pltpu.VMEM((2, half, DI), bf16),
            pltpu.VMEM((2, half, DI), bf16),
            pltpu.VMEM((half, DI), f32),
        ],
        compiler_params=pltpu.CompilerParams(vmem_limit_bytes=56 * 2**20),
        cost_estimate=pl.CostEstimate(
            flops=6 * half * half * 128 * 2 * MH,
            bytes_accessed=40 * half * DI,
            transcendentals=2 * MH * half * half,
        ),
        name="scan_backward",
    )(mixed, scan_grad, scan_out, dt, cum, cum_t, skip_row, states, carries)


def conv_block(previous, raw_rows, conv_weight, conv_bias):
    extended = jnp.concatenate([previous, raw_rows], axis=0)
    row_count = raw_rows.shape[0]
    running = conv_bias[None, :] + conv_weight[0][None, :] * extended[0:row_count]
    for offset in range(1, conv_weight.shape[0]):
        running = running + conv_weight[offset][None, :] * extended[offset : offset + row_count]
    return jax.nn.silu(running)


def local(
    tokens,
    cotangent,
    block_table,
    mixer_gain,
    in_proj,
    conv_weight,
    conv_bias,
    step_bias,
    decay_log,
    skip_gain,
    gated_gain,
    out_proj,
    attention_in,
    attention_out,
    feed_gain,
    gate_up,
    down_proj,
):
    ctx_count = lax.axis_size("ctx")
    my_index = lax.axis_index("ctx")
    is_last = my_index == ctx_count - 1
    device_rows = tokens.shape[1]
    half_rows = device_rows // 2
    lag_rows = KCONV - 1
    kv_width = KEY_VALUE_HEADS * HEAD_WIDTH
    slot_first = lax.dynamic_index_in_dim(block_table, 2 * my_index, keepdims=False)
    swapped = slot_first != my_index

    def arrange(value_rows):
        first_half = value_rows[:half_rows]
        second_half = value_rows[half_rows:]
        return jnp.concatenate(
            [
                jnp.where(swapped, second_half, first_half),
                jnp.where(swapped, first_half, second_half),
            ],
            axis=0,
        )

    block_ids = jnp.concatenate(
        [
            jnp.full((half_rows,), my_index, jnp.int32),
            jnp.full((half_rows,), 2 * ctx_count - 1 - my_index, jnp.int32),
        ]
    )
    token_positions = block_ids * half_rows + jnp.tile(jnp.arange(half_rows, dtype=jnp.int32), 2)
    freqs = jnp.exp(
        -(jnp.arange(HEAD_WIDTH // 2, dtype=f32) * (2.0 / HEAD_WIDTH)) * jnp.log(rope_base)
    )
    angles = token_positions.astype(f32)[:, None] * freqs[None, :]
    sign = jnp.where(jnp.arange(2 * HEAD_WIDTH) % HEAD_WIDTH < HEAD_WIDTH // 2, -1.0, 1.0)
    cosine, sine = tie(jnp.tile(jnp.cos(angles), (1, 4)), jnp.tile(jnp.sin(angles), (1, 4)) * sign)
    hidden = arrange(tokens[0]).astype(f32)
    out_grad = arrange(cotangent[0]).astype(f32)

    full_qkv = gather_weight(attention_in, True)
    full_in = gather_weight(in_proj, True)
    full_in, out_proj, attention_out, gate_up, down_proj = lax.optimization_barrier(
        (full_in, out_proj, attention_out, gate_up, down_proj)
    )
    full_out = gather_weight(out_proj, False)
    full_output_weight = gather_weight(attention_out, False)
    full_gu = gather_weight(gate_up, False)
    full_down = gather_weight(down_proj, False)

    scale_one = norm_scale(hidden)
    normed_one = (hidden * scale_one * mixer_gain).astype(bf16)

    qkv_rows = matmul(normed_one, full_qkv)
    q_t, pairs = prepare(qkv_rows, cosine, sine)
    all_pairs = gather_ctx(pairs).reshape(2 * ctx_count, half_rows, 2 * kv_width)
    table = pair_table(ctx_count, my_index)
    query_row = jnp.tile(jnp.arange(half_rows, dtype=jnp.int32), GROUP)[None]
    attn_low, attn_t, log_total = attn_forward(table, q_t, all_pairs, query_row)

    projected = matmul(normed_one, full_in)
    raw_conv = projected[:, DI : DI + CONV]
    step_raw = projected[:, DI + CONV :]
    early_tail = raw_conv[half_rows - lag_rows : half_rows]
    edges = jnp.concatenate([raw_conv[device_rows - lag_rows :], early_tail], axis=0)
    before, after = edge_exchange(edges.astype(bf16), lag_rows)
    prev_early = before.astype(f32)
    prev_late = jnp.where(is_last, early_tail, after.astype(f32))
    raw_early = raw_conv[:half_rows]
    raw_late = raw_conv[half_rows:]
    mixed = jnp.concatenate(
        [
            conv_block(prev_early, raw_early, conv_weight, conv_bias),
            conv_block(prev_late, raw_late, conv_weight, conv_bias),
        ],
        axis=0,
    )
    step_size = jax.nn.softplus(step_raw + step_bias[None, :])
    decay_rate = -jnp.exp(decay_log)
    dt = step_size.reshape(2, half_rows, MH)
    lower = jnp.tril(jnp.ones((half_rows, half_rows), f32))
    cum = jnp.einsum("ts,bsh->bth", lower, dt * decay_rate, precision=highest)
    cum_t = cum.swapaxes(1, 2)
    skip_row = jnp.repeat(skip_gain, MP)[None]
    part, updates = scan_forward(mixed, dt, cum, cum_t, skip_row)

    fades = gather_ctx(jnp.exp(cum[:, half_rows - 1]))
    fades = jnp.repeat(fades.reshape(2 * ctx_count, MH), MP, axis=1)
    block = jnp.arange(2 * ctx_count, dtype=jnp.int32)
    block_late = block >= ctx_count
    block_device = jnp.where(block_late, 2 * ctx_count - 1 - block, block)
    order = jnp.stack([block_device, block_device ^ my_index]) * 2 + block_late.astype(jnp.int32)
    states = exchange_states(order, updates, fades)
    gain_row = gated_gain[None]
    scan_out, gated_low = gated_forward(part, mixed, cum, states, projected, gain_row)

    mamba_out = matmul(gated_low, full_out)
    attn_out = matmul(attn_low, full_output_weight)
    second = hidden + mamba_out + attn_out
    scale_two = norm_scale(second)
    normed_two = (second * scale_two * feed_gain).astype(bf16)
    gate_rows = matmul(normed_two, full_gu)
    gate_part = gate_rows[:, :FF]
    up_part = gate_rows[:, FF:]
    sig_gate = jax.nn.sigmoid(gate_part)
    silu_gate = gate_part * sig_gate
    activated = (silu_gate * up_part).astype(bf16)
    result = second + matmul(activated, full_down)

    down_grad = out_grad.astype(bf16)
    down_part = row_contract(activated, down_grad)
    act_grad = backward_product(down_grad, full_down)
    gate_grad = act_grad * up_part * sig_gate * (1.0 + gate_part * (1.0 - sig_gate))
    up_grad = act_grad * silu_gate
    gu_grad = jnp.concatenate([gate_grad, up_grad], axis=1).astype(bf16)
    gu_part = rows_by_owner(row_contract(normed_two, gu_grad))
    d_model = hidden.shape[1]
    sum_1 = sum_core(
        [gu_part[..., k : k + d_model] for k in range(0, 2 * FF, d_model)] + [rows_by_owner(down_part)]
    )
    normed_two_grad = backward_product(gu_grad, full_gu)
    grad_feed = jnp.sum(normed_two_grad * second * scale_two, axis=0)
    resid_grad = out_grad + norm_backward(normed_two_grad * feed_gain, second, scale_two)
    branch_gradient = resid_grad.astype(bf16)
    gated_grad = backward_product(branch_gradient, full_out)
    scan_grad, z_grad, gain_parts, direct = gated_backward(
        gated_grad, scan_out, projected, gain_row, mixed, cum
    )
    grad_gated = jnp.sum(gain_parts[:, 0], axis=0)
    carries = exchange_states(order[:, ::-1], direct, fades)

    attn_grad = backward_product(branch_gradient, full_output_weight).astype(bf16)
    attn_grad, sum_1 = tie(attn_grad, sum_1)
    sum_1 = sum_first(sum_1)
    z_wide = row_contract(normed_one, z_grad[:, :d_model])
    z_rest = rows_by_owner(row_contract(normed_one, z_grad[:, d_model:]))
    rest_rows = z_rest.shape[4] // 2
    sum_2 = sum_core(
        [
            rows_by_owner(row_contract(gated_low, branch_gradient)),
            rows_by_owner(row_contract(attn_low, branch_gradient)),
            rows_by_owner(z_wide),
            jnp.concatenate([z_rest[..., :rest_rows, :], z_rest[..., rest_rows:, :]], axis=5),
        ]
    )
    dq, d_pairs = attn_backward(
        table, q_t, all_pairs, attn_grad, attn_t, log_total, cosine, sine, query_row
    )
    pair_grad = reduce_ctx(d_pairs.reshape(ctx_count, device_rows, 2 * kv_width))
    key_grad = pair_grad[:, :kv_width]
    quarter = HEAD_WIDTH // 2
    key_swapped = jnp.concatenate(
        [key_grad[:, k * quarter : (k + 1) * quarter] for k in (1, 0, 3, 2)], axis=1
    )
    qkv_grad = jnp.concatenate(
        [dq, (key_grad * cosine - key_swapped * sine).astype(bf16), pair_grad[:, kv_width:].astype(bf16)],
        axis=1,
    )

    scan_grad, sum_1, sum_2 = tie(scan_grad, sum_1, sum_2)
    sum_1 = sum_second(*sum_1)
    sum_2 = sum_first(sum_2)
    mixed_grad, d_cum, d_dt, skip_parts, last_parts = scan_backward(
        mixed, scan_grad, scan_out, dt, cum, cum_t, skip_row, states, carries
    )
    mixed_grad, sum_1, sum_2 = tie(mixed_grad, sum_1, sum_2)
    sum_1 = sum_last(sum_1)
    sum_2 = sum_second(*sum_2)
    grad_skip = jnp.sum(skip_parts.reshape(2, MH, MP), axis=(0, 2))
    last = jnp.sum(last_parts.reshape(2, MH, MP), axis=2)
    log_grad = jnp.einsum("ts,bth->bsh", lower, d_cum, precision=highest) + last[:, None, :]
    grad_decay = jnp.sum(log_grad * dt, axis=(0, 1)) * decay_rate
    step_grad = (d_dt + log_grad * decay_rate).reshape(device_rows, MH)
    step_raw_grad = step_grad * jax.nn.sigmoid(step_raw + step_bias[None, :])
    grad_step = jnp.sum(step_raw_grad, axis=0)
    _, conv_pull_early = jax.vjp(conv_block, prev_early, raw_early, conv_weight, conv_bias)
    prev_early_grad, raw_early_grad, weight_early_grad, bias_early_grad = conv_pull_early(
        mixed_grad[:half_rows]
    )
    _, conv_pull_late = jax.vjp(conv_block, prev_late, raw_late, conv_weight, conv_bias)
    prev_late_grad, raw_late_grad, weight_late_grad, bias_late_grad = conv_pull_late(
        mixed_grad[half_rows:]
    )
    backs = jnp.concatenate([prev_early_grad, prev_late_grad], axis=0)
    before_g, after_g = edge_exchange(backs.astype(bf16), lag_rows)
    early_tail_grad = after_g.astype(f32) + jnp.where(is_last, prev_late_grad, 0.0)
    late_tail_grad = before_g.astype(f32)
    raw_early_grad = raw_early_grad.at[half_rows - lag_rows :].add(early_tail_grad)
    raw_late_grad = raw_late_grad.at[half_rows - lag_rows :].add(late_tail_grad)
    raw_grad = jnp.concatenate([raw_early_grad, raw_late_grad], axis=0)
    raw_grad, sum_1, sum_2 = tie(raw_grad.astype(bf16), sum_1, sum_2)
    sum_2 = sum_last(sum_2)
    tail_width = CONV + MH
    tail_grad = jnp.concatenate(
        [raw_grad, step_raw_grad.astype(bf16), jnp.zeros((device_rows, -tail_width % 128), bf16), qkv_grad],
        axis=1,
    )
    sum_3 = sum_core([rows_by_owner(row_contract(normed_one, tail_grad))])
    sum_3 = sum_last(sum_second(*sum_first(sum_3)))
    normed_one_grad = (
        backward_product(qkv_grad, full_qkv)
        + backward_product(z_grad, full_in[:, :DI])
        + backward_product(tail_grad[:, :tail_width], full_in[:, DI:])
    )
    grad_mixer = jnp.sum(normed_one_grad * hidden * scale_one, axis=0)
    input_grad = resid_grad + norm_backward(normed_one_grad * mixer_gain, hidden, scale_one)

    small = (
        grad_mixer,
        grad_gated,
        grad_feed,
        (weight_early_grad + weight_late_grad).reshape(-1),
        bias_early_grad + bias_late_grad,
        grad_step,
        grad_decay,
        grad_skip,
    )
    each = d_model // (ctx_count * lax.axis_size("fsdp"))
    gu_blocks = 2 * FF // d_model
    grad_gu = jnp.concatenate([sum_1[k * each : (k + 1) * each] for k in range(gu_blocks)], axis=1)
    grad_down = sum_1[gu_blocks * each :]
    cuts = []
    for rows in (each * DI // d_model, each * QUERY_HEADS * HEAD_WIDTH // d_model, each, each // 2):
        cuts.append(sum_2[:rows])
        sum_2 = sum_2[rows:]
    grad_out, grad_o = cuts[:2]
    grad_in = jnp.concatenate(
        [
            cuts[2],
            jnp.concatenate([cuts[3][:, : d_model // 2], cuts[3][:, d_model // 2 :]], axis=0),
            sum_3[:, :tail_width],
        ],
        axis=1,
    )
    grad_qkv = sum_3[:, tail_width + -tail_width % 128 :]
    flat = jnp.concatenate(small)
    size = flat.shape[0]
    flat = jnp.pad(flat, (0, -size % 1024)).reshape(-1, 128)
    flat = all_sum(flat).reshape(-1)
    sums, start = [], 0
    for piece in small:
        sums.append(flat[start : start + piece.shape[0]])
        start += piece.shape[0]
    return (
        arrange(result).astype(bf16)[None],
        arrange(input_grad)[None],
        sums[0],
        grad_in,
        sums[3].reshape(conv_weight.shape),
        sums[4],
        sums[5],
        sums[6],
        sums[7],
        sums[1],
        grad_out,
        grad_qkv,
        grad_o,
        sums[2],
        grad_gu,
        grad_down,
    )


def solution(mesh):
    rows = P("fsdp", None)
    spread = P(("ctx", "fsdp"), None)
    tokens = P("fsdp", "ctx", None)
    return jax.shard_map(
        local,
        mesh=mesh,
        in_specs=(
            tokens, tokens, P(), P(), rows, P(), P(), P(), P(), P(), P(), rows, rows, rows, P(), rows, rows,
        ),
        out_specs=(
            tokens, tokens, P(), spread, P(), P(), P(), P(), P(), P(), spread, spread, spread, P(), spread, spread,
        ),
        check_vma=False,
    )
```

```python
import math

import jax
import jax.numpy as jnp
from jax import lax
from jax.experimental import pallas as pl
from jax.experimental.pallas import tpu as pltpu
from jax.sharding import PartitionSpec as P

DI = 1536
MH = 24
MP = 64
NS = 128
KCONV = 4
QUERY_HEADS = 8
KEY_VALUE_HEADS = 2
HEAD_WIDTH = 64
GROUP = QUERY_HEADS // KEY_VALUE_HEADS
FF = 2048
CONV = 1792
PAIRS = MH // 2

highest = lax.Precision.HIGHEST
epsilon = 1e-05
rope_base = 100000000000.0
score_scale = 0.125
masked_fill_value = -1e30
bf16 = jnp.bfloat16
f32 = jnp.float32


def xor_pairs(count, distance):
    return [(i, i ^ distance) for i in range(count)]


def swap(array, axis, distance):
    return lax.ppermute(array, axis, xor_pairs(lax.axis_size(axis), distance))


def norm_scale(value_rows):
    return lax.rsqrt(jnp.mean(value_rows * value_rows, axis=-1, keepdims=True) + epsilon)


def norm_backward(grad_norm, value_rows, scale):
    return scale * (
        grad_norm
        - value_rows * scale * scale * jnp.mean(grad_norm * value_rows, axis=-1, keepdims=True)
    )


def matmul(left, right):
    return jnp.dot(left, right, preferred_element_type=f32)


def row_contract(left, right):
    return lax.dot_general(left, right, (((0,), (0,)), ((), ())), preferred_element_type=f32)


def backward_product(grad_rows, weight):
    return lax.dot_general(grad_rows, weight, (((1,), (1,)), ((), ())), preferred_element_type=f32)


def edge_exchange(array, width):
    devices, length = lax.axis_size("ctx"), array.shape[0]
    up = [(i, i + 1) for i in range(devices - 1)]
    down = [(j, i) for i, j in up]
    before = lax.ppermute(array[length - width :], "ctx", up)
    after = lax.ppermute(array[:width], "ctx", down)
    return before, after


def swap_blocks(array, wanted, size):
    blocks = [array[:, k : k + size] for k in range(0, array.shape[1], size)]
    return jnp.where(wanted, jnp.concatenate([blocks[k ^ 1] for k in range(len(blocks))], axis=1), array)


def by_distance(rows):
    fs = lax.axis_index("fsdp")
    size = rows.shape[1] // 4
    return swap_blocks(swap_blocks(rows, fs // 2 == 1, 2 * size), fs % 2 == 1, size)


def gather_plain(weight):
    return lax.all_gather(weight, "fsdp", axis=0, tiled=True)


def gather_whole(weight):
    far = swap(weight, "fsdp", 2)
    return [weight, swap(weight, "fsdp", 1), far, swap(far, "fsdp", 1)]


def gather_outer(piece):
    return [piece] + [swap(piece, "ctx", k) for k in range(2, lax.axis_size("ctx"), 2)]


def pick(array, index, dim):
    return lax.dynamic_index_in_dim(array, index, dim, keepdims=False)


def sum_all(flat):
    rows, cols = flat.shape[4:]
    return lax.psum_scatter(
        flat.reshape(-1, cols), ("ctx", "fsdp"), scatter_dimension=0, tiled=True
    ).astype(f32)


def column_blocks(array, width):
    return [array[..., k : k + width] for k in range(0, array.shape[-1], width)]


def beside(rows, blocks):
    each = rows.shape[0] // blocks
    return jnp.concatenate([rows[k * each : (k + 1) * each] for k in range(blocks)], axis=1)


def exchange(array, dim, axis, stride, size):
    own = (lax.axis_index(axis) // stride) % size
    terms = [pick(array, own, dim)]
    for k in range(1, size):
        terms.append(swap(pick(array, own ^ k, dim), axis, k * stride))
    return terms


def add_up(terms):
    return sum(term.astype(f32) for term in terms)


def rows_by_owner(grad):
    ctx_count, fs_count = lax.axis_size("ctx"), lax.axis_size("fsdp")
    rows, cols = grad.shape
    return grad.astype(bf16).reshape(
        ctx_count // 2, 2, fs_count // 2, 2, rows // (ctx_count * fs_count), cols
    )


def sum_core(views):
    core = lax.axis_index("fsdp") % 2
    keep, send = (
        jnp.concatenate([pick(view, side, 3) for view in views], axis=3) for side in (core, 1 - core)
    )
    return (keep.astype(f32) + swap(send, "fsdp", 1).astype(f32)).astype(bf16)


def tie(*arrays):
    return lax.optimization_barrier(arrays)


def all_sum(array, axis, distance, limit):
    while distance < limit:
        array = array + swap(array, axis, distance)
        distance *= 2
    return array


def tail_sums(parts, small):
    ctx_count, fs_count = lax.axis_size("ctx"), lax.axis_size("fsdp")
    half, wide = parts.shape[0] // 2, fs_count // 2
    low = exchange(parts[:half], 2, "fsdp", 2, wide)
    high = exchange(parts[half:], 1, "ctx", 1, 2)
    small, *terms = tie(all_sum(small, "fsdp", 1, fs_count), *low, *high)
    low, high = (add_up(part).astype(bf16) for part in (terms[:wide], terms[wide:]))
    low = exchange(low, 1, "ctx", 1, 2)
    high = exchange(high, 1, "fsdp", 2, wide)
    small, *terms = tie(all_sum(small, "ctx", 1, 2), *low, *high)
    both = jnp.concatenate([add_up(part).astype(bf16) for part in (terms[:2], terms[2:])], axis=0)
    return add_up(exchange(both, 0, "ctx", 2, ctx_count // 2)), all_sum(small, "ctx", 2, ctx_count)


def pair_table(ctx_count, mine):
    step = jnp.arange(2 * ctx_count + 1, dtype=jnp.int32)
    late = step > mine
    key_block = jnp.where(late, step - (mine + 1), step)
    own = jnp.where(late, 2 * ctx_count - 1 - mine, mine)
    key_late = key_block >= ctx_count
    device = jnp.where(key_late, 2 * ctx_count - 1 - key_block, key_block)
    place = (device ^ mine) * 2 + key_late.astype(jnp.int32)
    return jnp.stack(
        [
            late.astype(jnp.int32),
            place,
            (key_block == 0).astype(jnp.int32),
            (key_block == own).astype(jnp.int32),
        ]
    )


def turn(x, cosine, sine):
    lane = lax.broadcasted_iota(jnp.int32, x.shape, 1) % HEAD_WIDTH
    swapped = jnp.where(
        lane < HEAD_WIDTH // 2,
        pltpu.roll(x, 2 * HEAD_WIDTH - HEAD_WIDTH // 2, 1),
        pltpu.roll(x, HEAD_WIDTH // 2, 1),
    )
    return x * cosine + swapped * sine


def side_by_side(rows):
    turned = [rows[:, 2 * HEAD_WIDTH * p : 2 * HEAD_WIDTH * (p + 1)].T for p in range(QUERY_HEADS // 2)]
    heads = [turned[h // 2][h % 2 * HEAD_WIDTH : (h % 2 + 1) * HEAD_WIDTH] for h in range(QUERY_HEADS)]
    return [
        jnp.concatenate(heads[g * GROUP : (g + 1) * GROUP], axis=1).astype(bf16)
        for g in range(KEY_VALUE_HEADS)
    ]


def head_pair(groups, pair):
    half = groups[0].shape[1] // GROUP
    heads = []
    for h in (2 * pair, 2 * pair + 1):
        k = h % GROUP
        heads.append(groups[h // GROUP][:, k * half : (k + 1) * half])
    return jnp.concatenate(heads, axis=0).T


def prepare_kernel(qkv_ref, cos_ref, sin_ref, q_ref, pair_ref):
    width = 2 * HEAD_WIDTH
    cosine, sine = cos_ref[...], sin_ref[...]
    queries = []
    for p in range(QUERY_HEADS // 2):
        turned = turn(qkv_ref[:, width * p : width * (p + 1)], cosine, sine)
        queries.append(turned.astype(bf16).astype(f32) * score_scale)
    for g, part in enumerate(side_by_side(jnp.concatenate(queries, axis=1))):
        q_ref[0, g] = part
    start = QUERY_HEADS * HEAD_WIDTH
    pair_ref[:, :width] = turn(qkv_ref[:, start : start + width], cosine, sine).astype(bf16)
    pair_ref[:, width:] = qkv_ref[:, start + width :].astype(bf16)


def prepare(qkv_rows, cosine, sine):
    half = qkv_rows.shape[0] // 2
    kv = KEY_VALUE_HEADS * HEAD_WIDTH
    turn_spec = pl.BlockSpec((half, 2 * HEAD_WIDTH), lambda b: (b, 0))
    return pl.pallas_call(
        prepare_kernel,
        grid=(2,),
        in_specs=[pl.BlockSpec((half, qkv_rows.shape[1]), lambda b: (b, 0)), turn_spec, turn_spec],
        out_specs=[
            pl.BlockSpec((1, KEY_VALUE_HEADS, HEAD_WIDTH, GROUP * half), lambda b: (b, 0, 0, 0)),
            pl.BlockSpec((half, 2 * kv), lambda b: (b, 0)),
        ],
        out_shape=[
            jax.ShapeDtypeStruct((2, KEY_VALUE_HEADS, HEAD_WIDTH, GROUP * half), bf16),
            jax.ShapeDtypeStruct((2 * half, 2 * kv), bf16),
        ],
        compiler_params=pltpu.CompilerParams(vmem_limit_bytes=24 * 2**20),
        cost_estimate=pl.CostEstimate(flops=2**22, bytes_accessed=2**22, transcendentals=0),
        name="prepare",
    )(qkv_rows, cosine, sine)


def attn_forward_kernel(tab, q_ref, kv_ref, row_ref, o_ref, ot_ref, lse_ref, m_s, l_s, acc_s):
    step = pl.program_id(0)
    diag = tab[3, step]

    @pl.when(tab[2, step] == 1)
    def _():
        m_s[...] = jnp.full(m_s.shape, masked_fill_value, f32)
        l_s[...] = jnp.zeros(l_s.shape, f32)
        acc_s[...] = jnp.zeros(acc_s.shape, f32)

    keys, queries = kv_ref.shape[1], q_ref.shape[3]
    limit = row_ref[...] + (1 - diag) * keys
    allowed = lax.broadcasted_iota(jnp.int32, (keys, queries), 0) <= limit
    kv = kv_ref[0]
    values_t = kv[:, KEY_VALUE_HEADS * HEAD_WIDTH :].astype(f32).T.astype(bf16)
    for g in range(KEY_VALUE_HEADS):
        head = slice(g * HEAD_WIDTH, (g + 1) * HEAD_WIDTH)
        scores = matmul(kv[:, head], q_ref[0, g])
        scores = jnp.where(allowed, scores, masked_fill_value)
        old = m_s[g]
        new = jnp.maximum(old, jnp.max(scores, axis=0, keepdims=True))
        probs = jnp.exp(scores - new)
        fade = jnp.exp(old - new)
        m_s[g] = new
        l_s[g] = l_s[g] * fade + jnp.sum(probs, axis=0, keepdims=True)
        acc_s[g] = acc_s[g] * fade + matmul(values_t[head], probs.astype(bf16))

    @pl.when(diag == 1)
    def _():
        outs = []
        for g in range(KEY_VALUE_HEADS):
            outs.append(acc_s[g] / l_s[g])
            ot_ref[0, g] = outs[g]
            lse_ref[0, g] = m_s[g] + jnp.log(l_s[g])
        for p in range(QUERY_HEADS // 2):
            o_ref[:, 2 * HEAD_WIDTH * p : 2 * HEAD_WIDTH * (p + 1)] = head_pair(outs, p).astype(bf16)


def attn_specs(half):
    width = GROUP * half
    query = pl.BlockSpec((1, KEY_VALUE_HEADS, HEAD_WIDTH, width), lambda j, t: (t[0, j], 0, 0, 0))
    row = pl.BlockSpec((1, KEY_VALUE_HEADS, 1, width), lambda j, t: (t[0, j], 0, 0, 0))
    pair = pl.BlockSpec((1, half, 2 * KEY_VALUE_HEADS * HEAD_WIDTH), lambda j, t: (t[1, j], 0, 0))
    natural = pl.BlockSpec((half, QUERY_HEADS * HEAD_WIDTH), lambda j, t: (t[0, j], 0))
    return query, row, pair, natural


def attn_forward(table, q_t, all_pairs, query_row):
    steps = table.shape[1]
    half, width = all_pairs.shape[1], q_t.shape[3]
    query, row, pair, natural = attn_specs(half)
    return pl.pallas_call(
        attn_forward_kernel,
        grid_spec=pltpu.PrefetchScalarGridSpec(
            num_scalar_prefetch=1,
            grid=(steps,),
            in_specs=[query, pair, pl.BlockSpec((1, width), lambda j, t: (0, 0))],
            out_specs=[natural, query, row],
            scratch_shapes=[
                pltpu.VMEM((KEY_VALUE_HEADS, 1, width), f32),
                pltpu.VMEM((KEY_VALUE_HEADS, 1, width), f32),
                pltpu.VMEM((KEY_VALUE_HEADS, HEAD_WIDTH, width), f32),
            ],
        ),
        out_shape=[
            jax.ShapeDtypeStruct((2 * half, QUERY_HEADS * HEAD_WIDTH), bf16),
            jax.ShapeDtypeStruct(q_t.shape, f32),
            jax.ShapeDtypeStruct((2, KEY_VALUE_HEADS, 1, width), f32),
        ],
        compiler_params=pltpu.CompilerParams(vmem_limit_bytes=40 * 2**20),
        cost_estimate=pl.CostEstimate(
            flops=steps * 4 * half * width * 2 * HEAD_WIDTH,
            bytes_accessed=2**23,
            transcendentals=steps * 2 * half * width,
        ),
        name="attn_forward",
    )(table, q_t, all_pairs, query_row)


def attn_backward_kernel(
    tab, q_ref, kv_ref, do_ref, ot_ref, lse_ref, cos_ref, sin_ref, row_ref,
    dq_ref, dkv_ref, do_s, dot_s, dq_s, dkv_s,
):
    step = pl.program_id(0)
    diag = tab[3, step]
    place = tab[1, step]

    @pl.when(step == 0)
    def _():
        dkv_s[...] = jnp.zeros(dkv_s.shape, f32)

    @pl.when(tab[2, step] == 1)
    def _():
        dq_s[...] = jnp.zeros(dq_s.shape, f32)
        for g, part in enumerate(side_by_side(do_ref[...].astype(f32))):
            do_s[g] = part
            dot_s[g] = jnp.sum(part.astype(f32) * ot_ref[0, g], axis=0, keepdims=True)

    keys, queries = kv_ref.shape[1], q_ref.shape[3]
    limit = row_ref[...] + (1 - diag) * keys
    allowed = lax.broadcasted_iota(jnp.int32, (keys, queries), 0) <= limit
    kv = kv_ref[0]
    kv_width = KEY_VALUE_HEADS * HEAD_WIDTH
    keys_t = kv[:, :kv_width].astype(f32).T.astype(bf16)
    grads = [None] * 4
    for g in range(KEY_VALUE_HEADS):
        head = slice(g * HEAD_WIDTH, (g + 1) * HEAD_WIDTH)
        v_head = slice(kv_width + g * HEAD_WIDTH, kv_width + (g + 1) * HEAD_WIDTH)
        q, d_out = q_ref[0, g], do_s[g]
        scores = matmul(kv[:, head], q)
        probs = jnp.exp(jnp.where(allowed, scores - lse_ref[0, g], masked_fill_value))
        d_probs = matmul(kv[:, v_head], d_out)
        d_scores = (probs * (d_probs - dot_s[g])).astype(bf16)
        dq_s[g] += matmul(keys_t[head], d_scores)
        grads[g] = backward_product(d_scores, q)
        grads[2 + g] = backward_product(probs.astype(bf16), d_out)
    dkv_s[place] += jnp.concatenate(grads, axis=1)

    @pl.when(diag == 1)
    def _():
        parts = [dq_s[g] for g in range(KEY_VALUE_HEADS)]
        for p in range(QUERY_HEADS // 2):
            turned = turn(head_pair(parts, p), cos_ref[...], -sin_ref[...]) * score_scale
            dq_ref[:, 2 * HEAD_WIDTH * p : 2 * HEAD_WIDTH * (p + 1)] = turned.astype(bf16)

    @pl.when(step == pl.num_programs(0) - 1)
    def _():
        dkv_ref[...] = dkv_s[...].astype(bf16)


def attn_backward(table, q_t, all_pairs, d_out, out_t, lse, cosine, sine, query_row):
    steps = table.shape[1]
    blocks, half, kv = all_pairs.shape
    width = q_t.shape[3]
    query, row, pair, natural = attn_specs(half)
    turn_spec = pl.BlockSpec((half, 2 * HEAD_WIDTH), lambda j, t: (t[0, j], 0))
    return pl.pallas_call(
        attn_backward_kernel,
        grid_spec=pltpu.PrefetchScalarGridSpec(
            num_scalar_prefetch=1,
            grid=(steps,),
            in_specs=[
                query, pair, natural, query, row, turn_spec, turn_spec,
                pl.BlockSpec((1, width), lambda j, t: (0, 0)),
            ],
            out_specs=[natural, pl.BlockSpec((blocks, half, kv), lambda j, t: (0, 0, 0))],
            scratch_shapes=[
                pltpu.VMEM((KEY_VALUE_HEADS, HEAD_WIDTH, width), bf16),
                pltpu.VMEM((KEY_VALUE_HEADS, 1, width), f32),
                pltpu.VMEM((KEY_VALUE_HEADS, HEAD_WIDTH, width), f32),
                pltpu.VMEM((blocks, half, kv), f32),
            ],
        ),
        out_shape=[
            jax.ShapeDtypeStruct((2 * half, QUERY_HEADS * HEAD_WIDTH), bf16),
            jax.ShapeDtypeStruct((blocks, half, kv), bf16),
        ],
        compiler_params=pltpu.CompilerParams(vmem_limit_bytes=56 * 2**20),
        cost_estimate=pl.CostEstimate(
            flops=steps * 10 * half * width * 2 * HEAD_WIDTH,
            bytes_accessed=2**24,
            transcendentals=steps * 2 * half * width,
        ),
        name="attn_backward",
    )(table, q_t, all_pairs, d_out, out_t, lse, cosine, sine, query_row)


def two_halves(values):
    high = values.astype(bf16)
    return high, (values - high.astype(f32)).astype(bf16)


def wide_product(left, right):
    return backward_product(
        jnp.concatenate([left[0], left[0], left[1]], axis=1),
        jnp.concatenate([right[0], right[1], right[0]], axis=1),
    )


def by_pair(columns, pair, left):
    return jnp.where(left, columns[:, 2 * pair : 2 * pair + 1], columns[:, 2 * pair + 1 : 2 * pair + 2])


def pair_lanes(pair):
    return slice(2 * MP * pair, 2 * MP * (pair + 1))


def scan_forward_kernel(m_ref, dt_ref, cum_ref, cumt_ref, skip_ref, part_ref, upd_ref, tail_s):
    half = m_ref.shape[0]
    left = lax.broadcasted_iota(jnp.int32, (half, 2 * MP), 1) < MP
    causal = lax.broadcasted_iota(jnp.int32, (half, half), 0) >= lax.broadcasted_iota(
        jnp.int32, (half, half), 1
    )
    b_rows = m_ref[:, DI : DI + NS].astype(bf16)
    scores = wide_product(two_halves(m_ref[:, DI + NS :]), two_halves(m_ref[:, DI : DI + NS]))
    dt, cum, cum_t = dt_ref[0], cum_ref[0], cumt_ref[0]
    tail = jnp.exp(cum[half - 1 : half, :] - cum)
    for pair in range(PAIRS):
        lanes = pair_lanes(pair)
        x = m_ref[:, lanes]
        scaled = x * by_pair(dt, pair, left)
        scaled_both = jnp.concatenate(two_halves(scaled), axis=1)
        outs = []
        for h in (2 * pair, 2 * pair + 1):
            gap = cum[:, h : h + 1] - cum_t[h : h + 1, :]
            weights = jnp.exp(jnp.where(causal, gap, masked_fill_value)) * scores
            high, rest = two_halves(weights)
            wide = matmul(high, scaled_both)
            outs.append(wide[:, : 2 * MP] + wide[:, 2 * MP :] + matmul(rest, scaled_both[:, : 2 * MP]))
        part_ref[:, lanes] = jnp.where(left, outs[0], outs[1]) + skip_ref[:, lanes] * x
        tail_s[:, lanes] = (scaled * by_pair(tail, pair, left)).astype(bf16)
    upd_ref[0] = row_contract(b_rows, tail_s[...]).astype(bf16)


def token_specs(half):
    per_block = pl.BlockSpec((1, half, MH), lambda b: (b, 0, 0))
    per_block_t = pl.BlockSpec((1, MH, half), lambda b: (b, 0, 0))
    return per_block, per_block_t


def scan_forward(mixed, dt, cum, cum_t, skip_row):
    half = mixed.shape[0] // 2
    per_block, per_block_t = token_specs(half)
    return pl.pallas_call(
        scan_forward_kernel,
        grid=(2,),
        in_specs=[
            pl.BlockSpec((half, CONV), lambda b: (b, 0)),
            per_block,
            per_block,
            per_block_t,
            pl.BlockSpec((1, DI), lambda b: (0, 0)),
        ],
        out_specs=[
            pl.BlockSpec((half, DI), lambda b: (b, 0)),
            pl.BlockSpec((1, NS, DI), lambda b: (b, 0, 0)),
        ],
        out_shape=[
            jax.ShapeDtypeStruct((2 * half, DI), f32),
            jax.ShapeDtypeStruct((2, NS, DI), bf16),
        ],
        scratch_shapes=[pltpu.VMEM((half, DI), bf16)],
        compiler_params=pltpu.CompilerParams(vmem_limit_bytes=48 * 2**20),
        cost_estimate=pl.CostEstimate(
            flops=2 * half * half * 128 * 2 * MH,
            bytes_accessed=16 * half * DI,
            transcendentals=2 * MH * half * half,
        ),
        name="scan_forward",
    )(mixed, dt, cum, cum_t, skip_row)


def state_kernel(order, upd_ref, fade_ref, out_ref):
    def one(i, state):
        place = order[i]
        out_ref[place] = state.astype(bf16)
        return state * fade_ref[pl.ds(place, 1), :] + upd_ref[place].astype(f32)

    lax.fori_loop(0, upd_ref.shape[0], one, jnp.zeros(upd_ref.shape[1:], f32))


def run_states(order, updates, fades):
    return pl.pallas_call(
        state_kernel,
        grid_spec=pltpu.PrefetchScalarGridSpec(
            num_scalar_prefetch=1,
            grid=(1,),
            in_specs=[
                pl.BlockSpec(updates.shape, lambda j, t: (0, 0, 0)),
                pl.BlockSpec(fades.shape, lambda j, t: (0, 0)),
            ],
            out_specs=pl.BlockSpec(updates.shape, lambda j, t: (0, 0, 0)),
        ),
        out_shape=jax.ShapeDtypeStruct(updates.shape, bf16),
        compiler_params=pltpu.CompilerParams(vmem_limit_bytes=24 * 2**20),
        name="run_states",
    )(order, updates, fades)


def send_updates(updates):
    count = lax.axis_size("ctx")
    share = NS // count
    parts = updates.reshape(2, count, share, DI).swapaxes(0, 1)
    return lax.all_to_all(parts, "ctx", 0, 0).reshape(2 * count, share, DI)


def return_states(states):
    count = lax.axis_size("ctx")
    back = lax.all_to_all(states.reshape(count, 2, NS // count, DI), "ctx", 0, 0)
    return back.swapaxes(0, 1).reshape(2, NS, DI)


def gated_forward_kernel(part_ref, c_ref, cum_ref, state_ref, z_ref, gain_ref, y_ref, low_ref, g_s):
    half = part_ref.shape[0]
    left = lax.broadcasted_iota(jnp.int32, (half, 2 * MP), 1) < MP
    c_rows, c_rest = two_halves(c_ref[...])
    carried = matmul(c_rows, state_ref[0]) + matmul(c_rest, state_ref[0])
    decay = jnp.exp(cum_ref[0])
    square = jnp.zeros((half, 2 * MP), f32)
    for pair in range(PAIRS):
        lanes = pair_lanes(pair)
        y = part_ref[:, lanes] + carried[:, lanes] * by_pair(decay, pair, left)
        y_ref[:, lanes] = y
        gated = y * jax.nn.silu(z_ref[:, lanes])
        g_s[:, lanes] = gated
        square += gated * gated
    scale = lax.rsqrt(jnp.sum(square, axis=1, keepdims=True) * (1.0 / DI) + epsilon)
    low_ref[...] = (g_s[...] * scale * gain_ref[...]).astype(bf16)


def gated_forward(part, mixed, cum, states, projected, gain):
    half = part.shape[0] // 2
    per_block, _ = token_specs(half)
    wide = pl.BlockSpec((half, DI), lambda b: (b, 0))
    return pl.pallas_call(
        gated_forward_kernel,
        grid=(2,),
        in_specs=[
            wide,
            pl.BlockSpec((half, NS), lambda b: (b, (DI + NS) // NS)),
            per_block,
            pl.BlockSpec((1, NS, DI), lambda b: (b, 0, 0)),
            wide,
            pl.BlockSpec((1, DI), lambda b: (0, 0)),
        ],
        out_specs=[wide, wide],
        out_shape=[
            jax.ShapeDtypeStruct((2 * half, DI), f32),
            jax.ShapeDtypeStruct((2 * half, DI), bf16),
        ],
        scratch_shapes=[pltpu.VMEM((half, DI), f32)],
        compiler_params=pltpu.CompilerParams(vmem_limit_bytes=48 * 2**20),
        cost_estimate=pl.CostEstimate(
            flops=4 * half * NS * DI + 40 * half * DI,
            bytes_accessed=30 * half * DI,
            transcendentals=4 * half * DI,
        ),
        name="gated_forward",
    )(part, mixed, cum, states, projected, gain)


def gated_backward_kernel(
    gg_ref, y_ref, z_ref, gain_ref, c_ref, cum_ref, yg_ref, zg_ref, gain_g_ref, direct_ref, g_s, w_s
):
    half = gg_ref.shape[0]
    left = lax.broadcasted_iota(jnp.int32, (half, 2 * MP), 1) < MP
    decay = jnp.exp(cum_ref[0])
    square = jnp.zeros((half, 2 * MP), f32)
    cross = jnp.zeros((half, 2 * MP), f32)
    for pair in range(PAIRS):
        lanes = pair_lanes(pair)
        gated = y_ref[:, lanes] * jax.nn.silu(z_ref[:, lanes])
        g_s[:, lanes] = gated
        square += gated * gated
        cross += gg_ref[:, lanes] * gain_ref[:, lanes] * gated
    scale = lax.rsqrt(jnp.sum(square, axis=1, keepdims=True) * (1.0 / DI) + epsilon)
    mean = jnp.sum(cross, axis=1, keepdims=True) * (1.0 / DI)
    pull = scale * scale * scale * mean
    for pair in range(PAIRS):
        lanes = pair_lanes(pair)
        gated, grad, z = g_s[:, lanes], gg_ref[:, lanes], z_ref[:, lanes]
        gain_g_ref[0, :, lanes] = jnp.sum(grad * gated * scale, axis=0, keepdims=True)
        inner = scale * grad * gain_ref[:, lanes] - gated * pull
        sig = jax.nn.sigmoid(z)
        zg_ref[:, lanes] = (inner * y_ref[:, lanes] * sig * (1.0 + z * (1.0 - sig))).astype(bf16)
        grad_y = inner * z * sig
        yg_ref[:, lanes] = grad_y
        w_s[:, lanes] = (grad_y * by_pair(decay, pair, left)).astype(bf16)
    direct_ref[0] = row_contract(c_ref[...].astype(bf16), w_s[...]).astype(bf16)


def gated_backward(gated_grad, scan_out, projected, gain, mixed, cum):
    half = gated_grad.shape[0] // 2
    per_block, _ = token_specs(half)
    wide = pl.BlockSpec((half, DI), lambda b: (b, 0))
    return pl.pallas_call(
        gated_backward_kernel,
        grid=(2,),
        in_specs=[
            wide,
            wide,
            wide,
            pl.BlockSpec((1, DI), lambda b: (0, 0)),
            pl.BlockSpec((half, NS), lambda b: (b, (DI + NS) // NS)),
            per_block,
        ],
        out_specs=[
            wide,
            wide,
            pl.BlockSpec((1, 1, DI), lambda b: (b, 0, 0)),
            pl.BlockSpec((1, NS, DI), lambda b: (b, 0, 0)),
        ],
        out_shape=[
            jax.ShapeDtypeStruct((2 * half, DI), f32),
            jax.ShapeDtypeStruct((2 * half, DI), bf16),
            jax.ShapeDtypeStruct((2, 1, DI), f32),
            jax.ShapeDtypeStruct((2, NS, DI), bf16),
        ],
        scratch_shapes=[pltpu.VMEM((half, DI), f32), pltpu.VMEM((half, DI), bf16)],
        compiler_params=pltpu.CompilerParams(vmem_limit_bytes=48 * 2**20),
        cost_estimate=pl.CostEstimate(
            flops=4 * half * NS * DI + 60 * half * DI,
            bytes_accessed=40 * half * DI,
            transcendentals=8 * half * DI,
        ),
        name="gated_backward",
    )(gated_grad, scan_out, projected, gain, mixed, cum)


def split_sum(values, spread):
    high, rest = two_halves(values)
    return matmul(high, spread) + matmul(rest, spread)


def scan_backward_kernel(
    m_ref, gy_ref, y_ref, dt_ref, cum_ref, cumt_ref, skip_ref, state_ref, carry_ref,
    dm_ref, dcum_ref, ddt_ref, dskip_ref, last_ref, tail_s, grow_s, blt_s,
):
    half = m_ref.shape[0]
    left = lax.broadcasted_iota(jnp.int32, (half, 2 * MP), 1) < MP
    upper = lax.broadcasted_iota(jnp.int32, (half, half), 0) <= lax.broadcasted_iota(
        jnp.int32, (half, half), 1
    )
    b_rows, b_rest = two_halves(m_ref[:, DI : DI + NS])
    c_rows, c_rest = two_halves(m_ref[:, DI + NS :])
    scores_t = wide_product((b_rows, b_rest), (c_rows, c_rest))
    dt, cum, cum_t = dt_ref[0], cum_ref[0], cumt_ref[0]
    grow = jnp.exp(cum)
    tail = jnp.exp(cum[half - 1 : half, :] - cum)
    fade = grow[half - 1 : half, :]
    carry_low = carry_ref[0]
    blt_s[...] = matmul(b_rows, carry_low)
    d_scores_t = jnp.zeros((half, half), f32)
    d_cum = jnp.zeros((half, 2 * MP), f32)
    d_dt = jnp.zeros((half, 2 * MP), f32)
    lane_head = lax.broadcasted_iota(jnp.int32, (2 * MP, 2 * MP), 0) // MP
    column = lax.broadcasted_iota(jnp.int32, (2 * MP, 2 * MP), 1)
    for pair in range(PAIRS):
        lanes = pair_lanes(pair)
        x, gy = m_ref[:, lanes], gy_ref[:, lanes]
        dt_pair = by_pair(dt, pair, left)
        scaled = x * dt_pair
        gy_low, gy_rest = two_halves(gy)
        scaled_two = two_halves(scaled)
        nothing = jnp.zeros_like(gy_low)
        outs = []
        for k, h in enumerate((2 * pair, 2 * pair + 1)):
            gap = cum_t[h : h + 1, :] - cum[:, h : h + 1]
            decays = jnp.exp(jnp.where(upper, gap, masked_fill_value))
            outs.append(matmul((decays * scores_t).astype(bf16), gy_low))
            mine = [jnp.where(left, v, nothing) if k == 0 else jnp.where(left, nothing, v) for v in scaled_two]
            d_scores_t += wide_product(mine, (gy_low, gy_rest)) * decays
        tail_pair = by_pair(tail, pair, left)
        from_tail = tail_pair * blt_s[:, lanes]
        d_scaled = jnp.where(left, outs[0], outs[1]) + from_tail
        dm_ref[:, lanes] = dt_pair * d_scaled + skip_ref[:, lanes] * gy
        spread = (lane_head + 2 * pair == column).astype(bf16)
        skipped = x * gy
        d_cum += split_sum(gy * y_ref[:, lanes] - skip_ref[:, lanes] * skipped - scaled * d_scaled, spread)
        d_dt += split_sum(x * d_scaled, spread)
        dskip_ref[0, :, lanes] = jnp.sum(skipped, axis=0, keepdims=True)
        held = jnp.sum(state_ref[0][:, lanes].astype(f32) * carry_low[:, lanes].astype(f32), axis=0, keepdims=True)
        last_ref[0, :, lanes] = jnp.sum(scaled * from_tail, axis=0, keepdims=True) + held * by_pair(
            fade, pair, left[0:1]
        )
        tail_s[0, :, lanes], tail_s[1, :, lanes] = two_halves(scaled * tail_pair)
        grow_s[0, :, lanes], grow_s[1, :, lanes] = two_halves(gy * by_pair(grow, pair, left))
    d_low, d_rest = two_halves(d_scores_t)
    dm_ref[:, DI : DI + NS] = (
        matmul(d_low, c_rows)
        + matmul(d_low, c_rest)
        + matmul(d_rest, c_rows)
        + backward_product(tail_s[0], carry_low)
        + backward_product(tail_s[1], carry_low)
    )
    dm_ref[:, DI + NS :] = (
        row_contract(d_low, b_rows)
        + row_contract(d_low, b_rest)
        + row_contract(d_rest, b_rows)
        + backward_product(grow_s[0], state_ref[0])
        + backward_product(grow_s[1], state_ref[0])
    )
    dcum_ref[0] = d_cum[:, :MH]
    ddt_ref[0] = d_dt[:, :MH]


def scan_backward(mixed, scan_grad, scan_out, dt, cum, cum_t, skip_row, states, carries):
    half = mixed.shape[0] // 2
    per_block, per_block_t = token_specs(half)
    wide = pl.BlockSpec((half, DI), lambda b: (b, 0))
    full = pl.BlockSpec((half, CONV), lambda b: (b, 0))
    state = pl.BlockSpec((1, NS, DI), lambda b: (b, 0, 0))
    row = pl.BlockSpec((1, 1, DI), lambda b: (b, 0, 0))
    return pl.pallas_call(
        scan_backward_kernel,
        grid=(2,),
        in_specs=[
            full, wide, wide, per_block, per_block, per_block_t,
            pl.BlockSpec((1, DI), lambda b: (0, 0)), state, state,
        ],
        out_specs=[full, per_block, per_block, row, row],
        out_shape=[
            jax.ShapeDtypeStruct((2 * half, CONV), f32),
            jax.ShapeDtypeStruct((2, half, MH), f32),
            jax.ShapeDtypeStruct((2, half, MH), f32),
            jax.ShapeDtypeStruct((2, 1, DI), f32),
            jax.ShapeDtypeStruct((2, 1, DI), f32),
        ],
        scratch_shapes=[
            pltpu.VMEM((2, half, DI), bf16),
            pltpu.VMEM((2, half, DI), bf16),
            pltpu.VMEM((half, DI), f32),
        ],
        compiler_params=pltpu.CompilerParams(vmem_limit_bytes=56 * 2**20),
        cost_estimate=pl.CostEstimate(
            flops=6 * half * half * 128 * 2 * MH,
            bytes_accessed=40 * half * DI,
            transcendentals=2 * MH * half * half,
        ),
        name="scan_backward",
    )(mixed, scan_grad, scan_out, dt, cum, cum_t, skip_row, states, carries)


def branch_columns(gated, attended):
    shards = lax.axis_size("fsdp")
    one, two = gated.shape[1] // shards, attended.shape[1] // shards
    pieces = []
    for k in range(shards):
        pieces += [gated[:, k * one : (k + 1) * one], attended[:, k * two : (k + 1) * two]]
    return jnp.concatenate(pieces, axis=1)


def branch_split(columns, one, two):
    shards = lax.axis_size("fsdp")
    one, two = one // shards, two // shards
    starts = [k * (one + two) for k in range(shards)]
    return (
        jnp.concatenate([columns[:, k : k + one] for k in starts], axis=1),
        jnp.concatenate([columns[:, k + one : k + one + two] for k in starts], axis=1),
    )


def conv_block(previous, raw_rows, conv_weight, conv_bias):
    extended = jnp.concatenate([previous, raw_rows], axis=0)
    row_count = raw_rows.shape[0]
    running = conv_bias[None, :] + conv_weight[0][None, :] * extended[0:row_count]
    for offset in range(1, conv_weight.shape[0]):
        running = running + conv_weight[offset][None, :] * extended[offset : offset + row_count]
    return jax.nn.silu(running)


def local(
    tokens,
    cotangent,
    block_table,
    mixer_gain,
    in_proj,
    conv_weight,
    conv_bias,
    step_bias,
    decay_log,
    skip_gain,
    gated_gain,
    out_proj,
    attention_in,
    attention_out,
    feed_gain,
    gate_up,
    down_proj,
):
    ctx_count = lax.axis_size("ctx")
    my_index = lax.axis_index("ctx")
    is_last = my_index == ctx_count - 1
    device_rows = tokens.shape[1]
    half_rows = device_rows // 2
    lag_rows = KCONV - 1
    kv_width = KEY_VALUE_HEADS * HEAD_WIDTH
    slot_first = lax.dynamic_index_in_dim(block_table, 2 * my_index, keepdims=False)
    swapped = slot_first != my_index

    def arrange(value_rows):
        first_half = value_rows[:half_rows]
        second_half = value_rows[half_rows:]
        return jnp.concatenate(
            [
                jnp.where(swapped, second_half, first_half),
                jnp.where(swapped, first_half, second_half),
            ],
            axis=0,
        )

    block_ids = jnp.concatenate(
        [
            jnp.full((half_rows,), my_index, jnp.int32),
            jnp.full((half_rows,), 2 * ctx_count - 1 - my_index, jnp.int32),
        ]
    )
    token_positions = block_ids * half_rows + jnp.tile(jnp.arange(half_rows, dtype=jnp.int32), 2)
    freqs = jnp.exp(
        -(jnp.arange(HEAD_WIDTH // 2, dtype=f32) * (2.0 / HEAD_WIDTH)) * jnp.log(rope_base)
    )
    angles = token_positions.astype(f32)[:, None] * freqs[None, :]
    sign = jnp.where(jnp.arange(2 * HEAD_WIDTH) % HEAD_WIDTH < HEAD_WIDTH // 2, -1.0, 1.0)
    cosine, sine = tie(jnp.tile(jnp.cos(angles), (1, 4)), jnp.tile(jnp.sin(angles), (1, 4)) * sign)
    hidden = arrange(tokens[0]).astype(f32)
    out_grad = arrange(cotangent[0]).astype(f32)

    scale_one = norm_scale(hidden)
    normed_one = (hidden * scale_one * mixer_gain).astype(bf16)

    mixer_in, gate_in = in_proj[:, DI:], in_proj[:, :DI]
    branch_rows = jnp.concatenate([out_proj, attention_out], axis=0)
    if lax.axis_size("fsdp") == 4 and ctx_count % 2 == 0:
        qkv_parts = gather_whole(attention_in)
        mixer_in, qkv_parts[2] = tie(mixer_in, qkv_parts[2])
        in_parts = gather_whole(mixer_in)
        full_qkv, full_in = jnp.concatenate(qkv_parts), jnp.concatenate(in_parts)
        order_rows = by_distance
    else:
        full_qkv, full_in = gather_plain(attention_in), gather_plain(mixer_in)
        order_rows = lambda rows: rows
    full_gate_in = gather_plain(gate_in)
    full_branch = gather_plain(branch_rows)
    full_gu = gather_plain(gate_up)
    full_down = gather_plain(down_proj)
    normed_turned = order_rows(normed_one)

    qkv_rows = matmul(normed_turned, full_qkv)
    q_t, pairs = prepare(qkv_rows, cosine, sine)
    outer_pairs = gather_outer(pairs)
    table = pair_table(ctx_count, my_index)
    query_row = jnp.tile(jnp.arange(half_rows, dtype=jnp.int32), GROUP)[None]
    projected = matmul(normed_turned, full_in)
    raw_conv = projected[:, :CONV]
    step_raw = projected[:, CONV:]
    early_tail = raw_conv[half_rows - lag_rows : half_rows]
    edges = jnp.concatenate([raw_conv[device_rows - lag_rows :], early_tail], axis=0)
    before, after = edge_exchange(edges.astype(bf16), lag_rows)
    prev_early = before.astype(f32)
    prev_late = jnp.where(is_last, early_tail, after.astype(f32))
    raw_early = raw_conv[:half_rows]
    raw_late = raw_conv[half_rows:]
    mixed = jnp.concatenate(
        [
            conv_block(prev_early, raw_early, conv_weight, conv_bias),
            conv_block(prev_late, raw_late, conv_weight, conv_bias),
        ],
        axis=0,
    )
    mixed, *outer_pairs = tie(mixed, *outer_pairs)
    outer_pairs = jnp.stack(outer_pairs)
    inner_pairs = swap(outer_pairs, "ctx", 1)
    step_size = jax.nn.softplus(step_raw + step_bias[None, :])
    decay_rate = -jnp.exp(decay_log)
    dt = step_size.reshape(2, half_rows, MH)
    lower = jnp.tril(jnp.ones((half_rows, half_rows), f32))
    cum = jnp.einsum("ts,bsh->bth", lower, dt * decay_rate, precision=highest)
    cum_t = cum.swapaxes(1, 2)
    skip_row = jnp.repeat(skip_gain, MP)[None]
    fades = jnp.broadcast_to(jnp.exp(cum[:, half_rows - 1]), (ctx_count, 2, MH))
    fades = lax.all_to_all(fades, "ctx", 0, 0)
    fades = jnp.repeat(fades.reshape(2 * ctx_count, MH), MP, axis=1)
    part, updates = scan_forward(mixed, dt, cum, cum_t, skip_row)

    block = jnp.arange(2 * ctx_count, dtype=jnp.int32)
    block_late = block >= ctx_count
    block_device = jnp.where(block_late, 2 * ctx_count - 1 - block, block)
    order = block_device * 2 + block_late.astype(jnp.int32)
    updates, inner_pairs = tie(updates, inner_pairs)
    all_pairs = jnp.stack([outer_pairs, inner_pairs], axis=1)
    all_pairs = all_pairs.reshape(2 * ctx_count, half_rows, 2 * kv_width)
    pieces = send_updates(updates)
    gate_z, pieces = tie(matmul(normed_one, full_gate_in), pieces)
    states = return_states(run_states(order, pieces, fades))
    attn_low, attn_t, log_total = attn_forward(table, q_t, all_pairs, query_row)
    states, attn_low = tie(states, attn_low)
    gain_row = gated_gain[None]
    scan_out, gated_low = gated_forward(part, mixed, cum, states, gate_z, gain_row)

    second = hidden + matmul(branch_columns(gated_low, attn_low), full_branch)
    scale_two = norm_scale(second)
    normed_two = (second * scale_two * feed_gain).astype(bf16)
    gate_rows = matmul(normed_two, full_gu)
    gate_part = gate_rows[:, :FF]
    up_part = gate_rows[:, FF:]
    sig_gate = jax.nn.sigmoid(gate_part)
    silu_gate = gate_part * sig_gate
    activated = (silu_gate * up_part).astype(bf16)
    result = second + matmul(activated, full_down)

    down_grad = out_grad.astype(bf16)
    d_model = hidden.shape[1]
    down_part = rows_by_owner(row_contract(activated, down_grad))
    act_grad = backward_product(down_grad, full_down)
    gate_grad = act_grad * up_part * sig_gate * (1.0 + gate_part * (1.0 - sig_gate))
    up_grad = act_grad * silu_gate
    gu_grad = jnp.concatenate([gate_grad, up_grad], axis=1).astype(bf16)
    gu_parts = [
        rows_by_owner(row_contract(normed_two, gu_grad[:, k : k + d_model])) for k in range(0, 2 * FF, d_model)
    ]
    normed_two_grad = backward_product(gu_grad, full_gu)
    grad_feed = jnp.sum(normed_two_grad * second * scale_two, axis=0)
    resid_grad = out_grad + norm_backward(normed_two_grad * feed_gain, second, scale_two)
    branch_gradient = resid_grad.astype(bf16)
    gated_grad, attn_grad = branch_split(
        backward_product(branch_gradient, full_branch), DI, QUERY_HEADS * HEAD_WIDTH
    )
    scan_grad, z_grad, gain_parts, direct = gated_backward(
        gated_grad, scan_out, gate_z, gain_row, mixed, cum
    )
    grad_gated = jnp.sum(gain_parts[:, 0], axis=0)
    pieces = send_updates(direct)

    attn_grad, pieces = tie(attn_grad.astype(bf16), pieces)
    carries = return_states(run_states(order[::-1], pieces, fades))
    z_part = rows_by_owner(row_contract(normed_one, z_grad[:, :d_model]))
    z_rest = rows_by_owner(row_contract(normed_one, z_grad[:, d_model:]))
    z_half = z_rest.shape[4] // 2
    views = [
        rows_by_owner(row_contract(gated_low, branch_gradient)),
        rows_by_owner(row_contract(attn_low, branch_gradient)),
        z_part,
        jnp.concatenate([z_rest[..., :z_half, :], z_rest[..., z_half:, :]], axis=5),
    ]
    views = gu_parts + [down_part] + views
    attn_grad, flat = tie(attn_grad, jnp.concatenate(views, axis=4))
    sums = sum_all(flat)
    dq, d_pairs = attn_backward(
        table, q_t, all_pairs, attn_grad, attn_t, log_total, cosine, sine, query_row
    )
    d_pairs, carries = tie(d_pairs, carries)
    d_pairs = d_pairs.reshape(ctx_count // 2, 2, device_rows, 2 * kv_width)
    pairs_sent, scan_grad = tie(d_pairs[:, 1], scan_grad)
    pairs_came = swap(pairs_sent, "ctx", 1)
    mixed_grad, d_cum, d_dt, skip_parts, last_parts = scan_backward(
        mixed, scan_grad, scan_out, dt, cum, cum_t, skip_row, states, carries
    )
    grad_skip = jnp.sum(skip_parts.reshape(2, MH, MP), axis=(0, 2))
    last = jnp.sum(last_parts.reshape(2, MH, MP), axis=2)
    log_grad = jnp.einsum("ts,bth->bsh", lower, d_cum, precision=highest) + last[:, None, :]
    grad_decay = jnp.sum(log_grad * dt, axis=(0, 1)) * decay_rate
    step_grad = (d_dt + log_grad * decay_rate).reshape(device_rows, MH)
    step_raw_grad = step_grad * jax.nn.sigmoid(step_raw + step_bias[None, :])
    grad_step = jnp.sum(step_raw_grad, axis=0)
    _, conv_pull_early = jax.vjp(conv_block, prev_early, raw_early, conv_weight, conv_bias)
    prev_early_grad, raw_early_grad, weight_early_grad, bias_early_grad = conv_pull_early(
        mixed_grad[:half_rows]
    )
    _, conv_pull_late = jax.vjp(conv_block, prev_late, raw_late, conv_weight, conv_bias)
    prev_late_grad, raw_late_grad, weight_late_grad, bias_late_grad = conv_pull_late(
        mixed_grad[half_rows:]
    )
    backs = jnp.concatenate([prev_early_grad, prev_late_grad], axis=0)
    backs, pairs_came = tie(backs.astype(bf16), pairs_came)
    own_pairs = (d_pairs[:, 0].astype(f32) + pairs_came.astype(f32)).astype(bf16)
    pair_terms = [own_pairs[0]] + [swap(own_pairs[k // 2], "ctx", k) for k in range(2, ctx_count, 2)]
    before_g, after_g = edge_exchange(backs, lag_rows)
    early_tail_grad = after_g.astype(f32) + jnp.where(is_last, prev_late_grad, 0.0)
    late_tail_grad = before_g.astype(f32)
    raw_early_grad = raw_early_grad.at[half_rows - lag_rows :].add(early_tail_grad)
    raw_late_grad = raw_late_grad.at[half_rows - lag_rows :].add(late_tail_grad)
    raw_grad = jnp.concatenate([raw_early_grad, raw_late_grad], axis=0)
    raw_grad, *pair_terms = tie(raw_grad.astype(bf16), *pair_terms)
    pair_grad = sum(term.astype(f32) for term in pair_terms)
    key_grad = pair_grad[:, :kv_width]
    quarter = HEAD_WIDTH // 2
    key_swapped = jnp.concatenate(
        [key_grad[:, k * quarter : (k + 1) * quarter] for k in (1, 0, 3, 2)], axis=1
    )
    qkv_grad = jnp.concatenate(
        [dq, (key_grad * cosine - key_swapped * sine).astype(bf16), pair_grad[:, kv_width:].astype(bf16)],
        axis=1,
    )
    tail_width = CONV + MH
    tail_grad = jnp.concatenate(
        [raw_grad, step_raw_grad.astype(bf16), jnp.zeros((device_rows, -tail_width % 128), bf16), qkv_grad],
        axis=1,
    )
    sum_3 = sum_core([rows_by_owner(row_contract(normed_one, tail_grad))])
    normed_one_grad = order_rows(
        backward_product(qkv_grad, full_qkv) + backward_product(tail_grad[:, :tail_width], full_in)
    ) + backward_product(z_grad, full_gate_in)
    grad_mixer = jnp.sum(normed_one_grad * hidden * scale_one, axis=0)
    input_grad = resid_grad + norm_backward(normed_one_grad * mixer_gain, hidden, scale_one)

    small = (
        grad_mixer,
        grad_gated,
        grad_feed,
        (weight_early_grad + weight_late_grad).reshape(-1),
        bias_early_grad + bias_late_grad,
        grad_step,
        grad_decay,
        grad_skip,
    )
    flat = jnp.concatenate(small)
    size = flat.shape[0]
    flat = jnp.pad(flat, (0, -size % 1024)).reshape(-1, 128)
    sum_3, flat = tail_sums(sum_3, flat)
    flat = flat.reshape(-1)
    pieces, start = [], 0
    for view in views:
        pieces.append(sums[start : start + view.shape[4]])
        start += view.shape[4]
    grad_gu = jnp.concatenate(pieces[: len(gu_parts)], axis=1)
    grad_down, grad_out, grad_o, grad_z, z_rest = pieces[len(gu_parts) :]
    z_rest = jnp.concatenate([z_rest[:, : d_model // 2], z_rest[:, d_model // 2 :]], axis=0)
    grad_in = jnp.concatenate([grad_z, z_rest, sum_3[:, :tail_width]], axis=1)
    grad_qkv = sum_3[:, tail_width + -tail_width % 128 :]
    sums, start = [], 0
    for piece in small:
        sums.append(flat[start : start + piece.shape[0]])
        start += piece.shape[0]
    return (
        arrange(result).astype(bf16)[None],
        arrange(input_grad)[None],
        sums[0],
        grad_in,
        sums[3].reshape(conv_weight.shape),
        sums[4],
        sums[5],
        sums[6],
        sums[7],
        sums[1],
        grad_out,
        grad_qkv,
        grad_o,
        sums[2],
        grad_gu,
        grad_down,
    )


def solution(mesh):
    rows = P("fsdp", None)
    spread = P(("ctx", "fsdp"), None)
    tokens = P("fsdp", "ctx", None)
    return jax.shard_map(
        local,
        mesh=mesh,
        in_specs=(
            tokens, tokens, P(), P(), rows, P(), P(), P(), P(), P(), P(), rows, rows, rows, P(), rows, rows,
        ),
        out_specs=(
            tokens, tokens, P(), spread, P(), P(), P(), P(), P(), P(), spread, spread, spread, P(), spread, spread,
        ),
        check_vma=False,
    )
```

```python
import math

import jax
import jax.numpy as jnp
from jax import lax
from jax.experimental import pallas as pl
from jax.experimental.pallas import tpu as pltpu
from jax.sharding import PartitionSpec as P

DI = 1536
MH = 24
MP = 64
NS = 128
KCONV = 4
QUERY_HEADS = 8
KEY_VALUE_HEADS = 2
HEAD_WIDTH = 64
GROUP = QUERY_HEADS // KEY_VALUE_HEADS
FF = 2048
CONV = 1792
PAIRS = MH // 2

highest = lax.Precision.HIGHEST
epsilon = 1e-05
rope_base = 100000000000.0
score_scale = 0.125
masked_fill_value = -1e30
bf16 = jnp.bfloat16
f32 = jnp.float32


def xor_pairs(count, distance):
    return [(i, i ^ distance) for i in range(count)]


def swap(array, axis, distance):
    return lax.ppermute(array, axis, xor_pairs(lax.axis_size(axis), distance))


def norm_scale(value_rows):
    return lax.rsqrt(jnp.mean(value_rows * value_rows, axis=-1, keepdims=True) + epsilon)


def norm_backward(grad_norm, value_rows, scale):
    return scale * (
        grad_norm
        - value_rows * scale * scale * jnp.mean(grad_norm * value_rows, axis=-1, keepdims=True)
    )


def matmul(left, right):
    return jnp.dot(left, right, preferred_element_type=f32)


def row_contract(left, right):
    return lax.dot_general(left, right, (((0,), (0,)), ((), ())), preferred_element_type=f32)


def backward_product(grad_rows, weight):
    return lax.dot_general(grad_rows, weight, (((1,), (1,)), ((), ())), preferred_element_type=f32)


def edge_exchange(array, width):
    devices, length = lax.axis_size("ctx"), array.shape[0]
    up = [(i, i + 1) for i in range(devices - 1)]
    down = [(j, i) for i, j in up]
    before = lax.ppermute(array[length - width :], "ctx", up)
    after = lax.ppermute(array[:width], "ctx", down)
    return before, after


def swap_blocks(array, wanted, size):
    blocks = [array[:, k : k + size] for k in range(0, array.shape[1], size)]
    return jnp.where(wanted, jnp.concatenate([blocks[k ^ 1] for k in range(len(blocks))], axis=1), array)


def by_distance(rows):
    fs = lax.axis_index("fsdp")
    size = rows.shape[1] // 4
    return swap_blocks(swap_blocks(rows, fs // 2 == 1, 2 * size), fs % 2 == 1, size)


def gather_plain(weight):
    return lax.all_gather(weight, "fsdp", axis=0, tiled=True)


def gather_whole(weight):
    far = swap(weight, "fsdp", 2)
    return [weight, swap(weight, "fsdp", 1), far, swap(far, "fsdp", 1)]


def gather_outer(piece):
    return [piece] + [swap(piece, "ctx", k) for k in range(2, lax.axis_size("ctx"), 2)]


def pick(array, index, dim):
    return lax.dynamic_index_in_dim(array, index, dim, keepdims=False)


def sum_all(flat):
    rows, cols = flat.shape[4:]
    return lax.psum_scatter(
        flat.reshape(-1, cols), ("ctx", "fsdp"), scatter_dimension=0, tiled=True
    ).astype(f32)


def column_blocks(array, width):
    return [array[..., k : k + width] for k in range(0, array.shape[-1], width)]


def beside(rows, blocks):
    each = rows.shape[0] // blocks
    return jnp.concatenate([rows[k * each : (k + 1) * each] for k in range(blocks)], axis=1)


def exchange(array, dim, axis, stride, size):
    own = (lax.axis_index(axis) // stride) % size
    terms = [pick(array, own, dim)]
    for k in range(1, size):
        terms.append(swap(pick(array, own ^ k, dim), axis, k * stride))
    return terms


def add_up(terms):
    return sum(term.astype(f32) for term in terms)


def rows_by_owner(grad):
    ctx_count, fs_count = lax.axis_size("ctx"), lax.axis_size("fsdp")
    rows, cols = grad.shape
    return grad.astype(bf16).reshape(
        ctx_count // 2, 2, fs_count // 2, 2, rows // (ctx_count * fs_count), cols
    )


def send_core(view):
    core = lax.axis_index("fsdp") % 2
    return pick(view, core, 3), swap(pick(view, 1 - core, 3), "fsdp", 1)


def first_terms(terms):
    parts = add_up(terms).astype(bf16)
    half = parts.shape[0] // 2
    low = exchange(parts[:half], 2, "fsdp", 2, parts.shape[2])
    return low + exchange(parts[half:], 1, "ctx", 1, 2)


def second_terms(terms):
    low, high = (add_up(part).astype(bf16) for part in (terms[:-2], terms[-2:]))
    return exchange(low, 1, "ctx", 1, 2) + exchange(high, 1, "fsdp", 2, high.shape[1])


def last_terms(terms):
    both = jnp.concatenate([add_up(part).astype(bf16) for part in (terms[:2], terms[2:])], axis=0)
    return exchange(both, 0, "ctx", 2, both.shape[0])


def tie(*arrays):
    return lax.optimization_barrier(arrays)


def all_sum(array, axis, distance, limit):
    while distance < limit:
        array = array + swap(array, axis, distance)
        distance *= 2
    return array


def pair_table(ctx_count, mine):
    step = jnp.arange(2 * ctx_count + 1, dtype=jnp.int32)
    late = step > mine
    key_block = jnp.where(late, step - (mine + 1), step)
    own = jnp.where(late, 2 * ctx_count - 1 - mine, mine)
    key_late = key_block >= ctx_count
    device = jnp.where(key_late, 2 * ctx_count - 1 - key_block, key_block)
    place = (device ^ mine) * 2 + key_late.astype(jnp.int32)
    return jnp.stack(
        [
            late.astype(jnp.int32),
            place,
            (key_block == 0).astype(jnp.int32),
            (key_block == own).astype(jnp.int32),
        ]
    )


def turn(x, cosine, sine):
    lane = lax.broadcasted_iota(jnp.int32, x.shape, 1) % HEAD_WIDTH
    swapped = jnp.where(
        lane < HEAD_WIDTH // 2,
        pltpu.roll(x, 2 * HEAD_WIDTH - HEAD_WIDTH // 2, 1),
        pltpu.roll(x, HEAD_WIDTH // 2, 1),
    )
    return x * cosine + swapped * sine


def side_by_side(rows):
    turned = [rows[:, 2 * HEAD_WIDTH * p : 2 * HEAD_WIDTH * (p + 1)].T for p in range(QUERY_HEADS // 2)]
    heads = [turned[h // 2][h % 2 * HEAD_WIDTH : (h % 2 + 1) * HEAD_WIDTH] for h in range(QUERY_HEADS)]
    return [
        jnp.concatenate(heads[g * GROUP : (g + 1) * GROUP], axis=1).astype(bf16)
        for g in range(KEY_VALUE_HEADS)
    ]


def head_pair(groups, pair):
    half = groups[0].shape[1] // GROUP
    heads = []
    for h in (2 * pair, 2 * pair + 1):
        k = h % GROUP
        heads.append(groups[h // GROUP][:, k * half : (k + 1) * half])
    return jnp.concatenate(heads, axis=0).T


def prepare_kernel(qkv_ref, cos_ref, sin_ref, q_ref, pair_ref):
    width = 2 * HEAD_WIDTH
    cosine, sine = cos_ref[...], sin_ref[...]
    queries = []
    for p in range(QUERY_HEADS // 2):
        turned = turn(qkv_ref[:, width * p : width * (p + 1)], cosine, sine)
        queries.append(turned.astype(bf16).astype(f32) * score_scale)
    for g, part in enumerate(side_by_side(jnp.concatenate(queries, axis=1))):
        q_ref[0, g] = part
    start = QUERY_HEADS * HEAD_WIDTH
    pair_ref[:, :width] = turn(qkv_ref[:, start : start + width], cosine, sine).astype(bf16)
    pair_ref[:, width:] = qkv_ref[:, start + width :].astype(bf16)


def prepare(qkv_rows, cosine, sine):
    half = qkv_rows.shape[0] // 2
    kv = KEY_VALUE_HEADS * HEAD_WIDTH
    turn_spec = pl.BlockSpec((half, 2 * HEAD_WIDTH), lambda b: (b, 0))
    return pl.pallas_call(
        prepare_kernel,
        grid=(2,),
        in_specs=[pl.BlockSpec((half, qkv_rows.shape[1]), lambda b: (b, 0)), turn_spec, turn_spec],
        out_specs=[
            pl.BlockSpec((1, KEY_VALUE_HEADS, HEAD_WIDTH, GROUP * half), lambda b: (b, 0, 0, 0)),
            pl.BlockSpec((half, 2 * kv), lambda b: (b, 0)),
        ],
        out_shape=[
            jax.ShapeDtypeStruct((2, KEY_VALUE_HEADS, HEAD_WIDTH, GROUP * half), bf16),
            jax.ShapeDtypeStruct((2 * half, 2 * kv), bf16),
        ],
        compiler_params=pltpu.CompilerParams(vmem_limit_bytes=24 * 2**20),
        cost_estimate=pl.CostEstimate(flops=2**22, bytes_accessed=2**22, transcendentals=0),
        name="prepare",
    )(qkv_rows, cosine, sine)


def attn_forward_kernel(tab, q_ref, kv_ref, row_ref, o_ref, ot_ref, lse_ref, m_s, l_s, acc_s):
    step = pl.program_id(0)
    diag = tab[3, step]

    @pl.when(tab[2, step] == 1)
    def _():
        m_s[...] = jnp.full(m_s.shape, masked_fill_value, f32)
        l_s[...] = jnp.zeros(l_s.shape, f32)
        acc_s[...] = jnp.zeros(acc_s.shape, f32)

    keys, queries = kv_ref.shape[1], q_ref.shape[3]
    limit = row_ref[...] + (1 - diag) * keys
    allowed = lax.broadcasted_iota(jnp.int32, (keys, queries), 0) <= limit
    kv = kv_ref[0]
    values_t = kv[:, KEY_VALUE_HEADS * HEAD_WIDTH :].astype(f32).T.astype(bf16)
    for g in range(KEY_VALUE_HEADS):
        head = slice(g * HEAD_WIDTH, (g + 1) * HEAD_WIDTH)
        scores = matmul(kv[:, head], q_ref[0, g])
        scores = jnp.where(allowed, scores, masked_fill_value)
        old = m_s[g]
        new = jnp.maximum(old, jnp.max(scores, axis=0, keepdims=True))
        probs = jnp.exp(scores - new)
        fade = jnp.exp(old - new)
        m_s[g] = new
        l_s[g] = l_s[g] * fade + jnp.sum(probs, axis=0, keepdims=True)
        acc_s[g] = acc_s[g] * fade + matmul(values_t[head], probs.astype(bf16))

    @pl.when(diag == 1)
    def _():
        outs = []
        for g in range(KEY_VALUE_HEADS):
            outs.append(acc_s[g] / l_s[g])
            ot_ref[0, g] = outs[g]
            lse_ref[0, g] = m_s[g] + jnp.log(l_s[g])
        for p in range(QUERY_HEADS // 2):
            o_ref[:, 2 * HEAD_WIDTH * p : 2 * HEAD_WIDTH * (p + 1)] = head_pair(outs, p).astype(bf16)


def attn_specs(half):
    width = GROUP * half
    query = pl.BlockSpec((1, KEY_VALUE_HEADS, HEAD_WIDTH, width), lambda j, t: (t[0, j], 0, 0, 0))
    row = pl.BlockSpec((1, KEY_VALUE_HEADS, 1, width), lambda j, t: (t[0, j], 0, 0, 0))
    pair = pl.BlockSpec((1, half, 2 * KEY_VALUE_HEADS * HEAD_WIDTH), lambda j, t: (t[1, j], 0, 0))
    natural = pl.BlockSpec((half, QUERY_HEADS * HEAD_WIDTH), lambda j, t: (t[0, j], 0))
    return query, row, pair, natural


def attn_forward(table, q_t, all_pairs, query_row):
    steps = table.shape[1]
    half, width = all_pairs.shape[1], q_t.shape[3]
    query, row, pair, natural = attn_specs(half)
    return pl.pallas_call(
        attn_forward_kernel,
        grid_spec=pltpu.PrefetchScalarGridSpec(
            num_scalar_prefetch=1,
            grid=(steps,),
            in_specs=[query, pair, pl.BlockSpec((1, width), lambda j, t: (0, 0))],
            out_specs=[natural, query, row],
            scratch_shapes=[
                pltpu.VMEM((KEY_VALUE_HEADS, 1, width), f32),
                pltpu.VMEM((KEY_VALUE_HEADS, 1, width), f32),
                pltpu.VMEM((KEY_VALUE_HEADS, HEAD_WIDTH, width), f32),
            ],
        ),
        out_shape=[
            jax.ShapeDtypeStruct((2 * half, QUERY_HEADS * HEAD_WIDTH), bf16),
            jax.ShapeDtypeStruct(q_t.shape, f32),
            jax.ShapeDtypeStruct((2, KEY_VALUE_HEADS, 1, width), f32),
        ],
        compiler_params=pltpu.CompilerParams(vmem_limit_bytes=40 * 2**20),
        cost_estimate=pl.CostEstimate(
            flops=steps * 4 * half * width * 2 * HEAD_WIDTH,
            bytes_accessed=2**23,
            transcendentals=steps * 2 * half * width,
        ),
        name="attn_forward",
    )(table, q_t, all_pairs, query_row)


def attn_backward_kernel(
    tab, q_ref, kv_ref, do_ref, ot_ref, lse_ref, cos_ref, sin_ref, row_ref,
    dq_ref, dkv_ref, do_s, dot_s, dq_s, dkv_s,
):
    step = pl.program_id(0)
    diag = tab[3, step]
    place = tab[1, step]

    @pl.when(step == 0)
    def _():
        dkv_s[...] = jnp.zeros(dkv_s.shape, f32)

    @pl.when(tab[2, step] == 1)
    def _():
        dq_s[...] = jnp.zeros(dq_s.shape, f32)
        for g, part in enumerate(side_by_side(do_ref[...].astype(f32))):
            do_s[g] = part
            dot_s[g] = jnp.sum(part.astype(f32) * ot_ref[0, g], axis=0, keepdims=True)

    keys, queries = kv_ref.shape[1], q_ref.shape[3]
    limit = row_ref[...] + (1 - diag) * keys
    allowed = lax.broadcasted_iota(jnp.int32, (keys, queries), 0) <= limit
    kv = kv_ref[0]
    kv_width = KEY_VALUE_HEADS * HEAD_WIDTH
    keys_t = kv[:, :kv_width].astype(f32).T.astype(bf16)
    grads = [None] * 4
    for g in range(KEY_VALUE_HEADS):
        head = slice(g * HEAD_WIDTH, (g + 1) * HEAD_WIDTH)
        v_head = slice(kv_width + g * HEAD_WIDTH, kv_width + (g + 1) * HEAD_WIDTH)
        q, d_out = q_ref[0, g], do_s[g]
        scores = matmul(kv[:, head], q)
        probs = jnp.exp(jnp.where(allowed, scores - lse_ref[0, g], masked_fill_value))
        d_probs = matmul(kv[:, v_head], d_out)
        d_scores = (probs * (d_probs - dot_s[g])).astype(bf16)
        dq_s[g] += matmul(keys_t[head], d_scores)
        grads[g] = backward_product(d_scores, q)
        grads[2 + g] = backward_product(probs.astype(bf16), d_out)
    dkv_s[place] += jnp.concatenate(grads, axis=1)

    @pl.when(diag == 1)
    def _():
        parts = [dq_s[g] for g in range(KEY_VALUE_HEADS)]
        for p in range(QUERY_HEADS // 2):
            turned = turn(head_pair(parts, p), cos_ref[...], -sin_ref[...]) * score_scale
            dq_ref[:, 2 * HEAD_WIDTH * p : 2 * HEAD_WIDTH * (p + 1)] = turned.astype(bf16)

    @pl.when(step == pl.num_programs(0) - 1)
    def _():
        dkv_ref[...] = dkv_s[...].astype(bf16)


def attn_backward(table, q_t, all_pairs, d_out, out_t, lse, cosine, sine, query_row):
    steps = table.shape[1]
    blocks, half, kv = all_pairs.shape
    width = q_t.shape[3]
    query, row, pair, natural = attn_specs(half)
    turn_spec = pl.BlockSpec((half, 2 * HEAD_WIDTH), lambda j, t: (t[0, j], 0))
    return pl.pallas_call(
        attn_backward_kernel,
        grid_spec=pltpu.PrefetchScalarGridSpec(
            num_scalar_prefetch=1,
            grid=(steps,),
            in_specs=[
                query, pair, natural, query, row, turn_spec, turn_spec,
                pl.BlockSpec((1, width), lambda j, t: (0, 0)),
            ],
            out_specs=[natural, pl.BlockSpec((blocks, half, kv), lambda j, t: (0, 0, 0))],
            scratch_shapes=[
                pltpu.VMEM((KEY_VALUE_HEADS, HEAD_WIDTH, width), bf16),
                pltpu.VMEM((KEY_VALUE_HEADS, 1, width), f32),
                pltpu.VMEM((KEY_VALUE_HEADS, HEAD_WIDTH, width), f32),
                pltpu.VMEM((blocks, half, kv), f32),
            ],
        ),
        out_shape=[
            jax.ShapeDtypeStruct((2 * half, QUERY_HEADS * HEAD_WIDTH), bf16),
            jax.ShapeDtypeStruct((blocks, half, kv), bf16),
        ],
        compiler_params=pltpu.CompilerParams(vmem_limit_bytes=56 * 2**20),
        cost_estimate=pl.CostEstimate(
            flops=steps * 10 * half * width * 2 * HEAD_WIDTH,
            bytes_accessed=2**24,
            transcendentals=steps * 2 * half * width,
        ),
        name="attn_backward",
    )(table, q_t, all_pairs, d_out, out_t, lse, cosine, sine, query_row)


def two_halves(values):
    high = values.astype(bf16)
    return high, (values - high.astype(f32)).astype(bf16)


def wide_product(left, right):
    return backward_product(
        jnp.concatenate([left[0], left[0], left[1]], axis=1),
        jnp.concatenate([right[0], right[1], right[0]], axis=1),
    )


def by_pair(columns, pair, left):
    return jnp.where(left, columns[:, 2 * pair : 2 * pair + 1], columns[:, 2 * pair + 1 : 2 * pair + 2])


def pair_lanes(pair):
    return slice(2 * MP * pair, 2 * MP * (pair + 1))


def scan_forward_kernel(m_ref, dt_ref, cum_ref, cumt_ref, skip_ref, part_ref, upd_ref, tail_s):
    half = m_ref.shape[0]
    left = lax.broadcasted_iota(jnp.int32, (half, 2 * MP), 1) < MP
    causal = lax.broadcasted_iota(jnp.int32, (half, half), 0) >= lax.broadcasted_iota(
        jnp.int32, (half, half), 1
    )
    b_rows = m_ref[:, DI : DI + NS].astype(bf16)
    scores = wide_product(two_halves(m_ref[:, DI + NS :]), two_halves(m_ref[:, DI : DI + NS]))
    dt, cum, cum_t = dt_ref[0], cum_ref[0], cumt_ref[0]
    tail = jnp.exp(cum[half - 1 : half, :] - cum)
    for pair in range(PAIRS):
        lanes = pair_lanes(pair)
        x = m_ref[:, lanes]
        scaled = x * by_pair(dt, pair, left)
        scaled_both = jnp.concatenate(two_halves(scaled), axis=1)
        outs = []
        for h in (2 * pair, 2 * pair + 1):
            gap = cum[:, h : h + 1] - cum_t[h : h + 1, :]
            weights = jnp.exp(jnp.where(causal, gap, masked_fill_value)) * scores
            high, rest = two_halves(weights)
            wide = matmul(high, scaled_both)
            outs.append(wide[:, : 2 * MP] + wide[:, 2 * MP :] + matmul(rest, scaled_both[:, : 2 * MP]))
        part_ref[:, lanes] = jnp.where(left, outs[0], outs[1]) + skip_ref[:, lanes] * x
        tail_s[:, lanes] = (scaled * by_pair(tail, pair, left)).astype(bf16)
    upd_ref[0] = row_contract(b_rows, tail_s[...]).astype(bf16)


def token_specs(half):
    per_block = pl.BlockSpec((1, half, MH), lambda b: (b, 0, 0))
    per_block_t = pl.BlockSpec((1, MH, half), lambda b: (b, 0, 0))
    return per_block, per_block_t


def scan_forward(mixed, dt, cum, cum_t, skip_row):
    half = mixed.shape[0] // 2
    per_block, per_block_t = token_specs(half)
    return pl.pallas_call(
        scan_forward_kernel,
        grid=(2,),
        in_specs=[
            pl.BlockSpec((half, CONV), lambda b: (b, 0)),
            per_block,
            per_block,
            per_block_t,
            pl.BlockSpec((1, DI), lambda b: (0, 0)),
        ],
        out_specs=[
            pl.BlockSpec((half, DI), lambda b: (b, 0)),
            pl.BlockSpec((1, NS, DI), lambda b: (b, 0, 0)),
        ],
        out_shape=[
            jax.ShapeDtypeStruct((2 * half, DI), f32),
            jax.ShapeDtypeStruct((2, NS, DI), bf16),
        ],
        scratch_shapes=[pltpu.VMEM((half, DI), bf16)],
        compiler_params=pltpu.CompilerParams(vmem_limit_bytes=48 * 2**20),
        cost_estimate=pl.CostEstimate(
            flops=2 * half * half * 128 * 2 * MH,
            bytes_accessed=16 * half * DI,
            transcendentals=2 * MH * half * half,
        ),
        name="scan_forward",
    )(mixed, dt, cum, cum_t, skip_row)


def state_kernel(order, upd_ref, fade_ref, out_ref):
    def one(i, state):
        place = order[i]
        out_ref[place] = state.astype(bf16)
        return state * fade_ref[pl.ds(place, 1), :] + upd_ref[place].astype(f32)

    lax.fori_loop(0, upd_ref.shape[0], one, jnp.zeros(upd_ref.shape[1:], f32))


def run_states(order, updates, fades):
    return pl.pallas_call(
        state_kernel,
        grid_spec=pltpu.PrefetchScalarGridSpec(
            num_scalar_prefetch=1,
            grid=(1,),
            in_specs=[
                pl.BlockSpec(updates.shape, lambda j, t: (0, 0, 0)),
                pl.BlockSpec(fades.shape, lambda j, t: (0, 0)),
            ],
            out_specs=pl.BlockSpec(updates.shape, lambda j, t: (0, 0, 0)),
        ),
        out_shape=jax.ShapeDtypeStruct(updates.shape, bf16),
        compiler_params=pltpu.CompilerParams(vmem_limit_bytes=24 * 2**20),
        name="run_states",
    )(order, updates, fades)


def send_updates(updates):
    count = lax.axis_size("ctx")
    share = NS // count
    parts = updates.reshape(2, count, share, DI).swapaxes(0, 1)
    return lax.all_to_all(parts, "ctx", 0, 0).reshape(2 * count, share, DI)


def return_states(states):
    count = lax.axis_size("ctx")
    back = lax.all_to_all(states.reshape(count, 2, NS // count, DI), "ctx", 0, 0)
    return back.swapaxes(0, 1).reshape(2, NS, DI)


def gated_forward_kernel(part_ref, c_ref, cum_ref, state_ref, z_ref, gain_ref, y_ref, low_ref, g_s):
    half = part_ref.shape[0]
    left = lax.broadcasted_iota(jnp.int32, (half, 2 * MP), 1) < MP
    c_rows, c_rest = two_halves(c_ref[...])
    carried = matmul(c_rows, state_ref[0]) + matmul(c_rest, state_ref[0])
    decay = jnp.exp(cum_ref[0])
    square = jnp.zeros((half, 2 * MP), f32)
    for pair in range(PAIRS):
        lanes = pair_lanes(pair)
        y = part_ref[:, lanes] + carried[:, lanes] * by_pair(decay, pair, left)
        y_ref[:, lanes] = y
        gated = y * jax.nn.silu(z_ref[:, lanes])
        g_s[:, lanes] = gated
        square += gated * gated
    scale = lax.rsqrt(jnp.sum(square, axis=1, keepdims=True) * (1.0 / DI) + epsilon)
    low_ref[...] = (g_s[...] * scale * gain_ref[...]).astype(bf16)


def gated_forward(part, mixed, cum, states, projected, gain):
    half = part.shape[0] // 2
    per_block, _ = token_specs(half)
    wide = pl.BlockSpec((half, DI), lambda b: (b, 0))
    return pl.pallas_call(
        gated_forward_kernel,
        grid=(2,),
        in_specs=[
            wide,
            pl.BlockSpec((half, NS), lambda b: (b, (DI + NS) // NS)),
            per_block,
            pl.BlockSpec((1, NS, DI), lambda b: (b, 0, 0)),
            wide,
            pl.BlockSpec((1, DI), lambda b: (0, 0)),
        ],
        out_specs=[wide, wide],
        out_shape=[
            jax.ShapeDtypeStruct((2 * half, DI), f32),
            jax.ShapeDtypeStruct((2 * half, DI), bf16),
        ],
        scratch_shapes=[pltpu.VMEM((half, DI), f32)],
        compiler_params=pltpu.CompilerParams(vmem_limit_bytes=48 * 2**20),
        cost_estimate=pl.CostEstimate(
            flops=4 * half * NS * DI + 40 * half * DI,
            bytes_accessed=30 * half * DI,
            transcendentals=4 * half * DI,
        ),
        name="gated_forward",
    )(part, mixed, cum, states, projected, gain)


def gated_backward_kernel(
    gg_ref, y_ref, z_ref, gain_ref, c_ref, cum_ref, yg_ref, zg_ref, gain_g_ref, direct_ref, g_s, w_s
):
    half = gg_ref.shape[0]
    left = lax.broadcasted_iota(jnp.int32, (half, 2 * MP), 1) < MP
    decay = jnp.exp(cum_ref[0])
    square = jnp.zeros((half, 2 * MP), f32)
    cross = jnp.zeros((half, 2 * MP), f32)
    for pair in range(PAIRS):
        lanes = pair_lanes(pair)
        gated = y_ref[:, lanes] * jax.nn.silu(z_ref[:, lanes])
        g_s[:, lanes] = gated
        square += gated * gated
        cross += gg_ref[:, lanes] * gain_ref[:, lanes] * gated
    scale = lax.rsqrt(jnp.sum(square, axis=1, keepdims=True) * (1.0 / DI) + epsilon)
    mean = jnp.sum(cross, axis=1, keepdims=True) * (1.0 / DI)
    pull = scale * scale * scale * mean
    for pair in range(PAIRS):
        lanes = pair_lanes(pair)
        gated, grad, z = g_s[:, lanes], gg_ref[:, lanes], z_ref[:, lanes]
        gain_g_ref[0, :, lanes] = jnp.sum(grad * gated * scale, axis=0, keepdims=True)
        inner = scale * grad * gain_ref[:, lanes] - gated * pull
        sig = jax.nn.sigmoid(z)
        zg_ref[:, lanes] = (inner * y_ref[:, lanes] * sig * (1.0 + z * (1.0 - sig))).astype(bf16)
        grad_y = inner * z * sig
        yg_ref[:, lanes] = grad_y
        w_s[:, lanes] = (grad_y * by_pair(decay, pair, left)).astype(bf16)
    direct_ref[0] = row_contract(c_ref[...].astype(bf16), w_s[...]).astype(bf16)


def gated_backward(gated_grad, scan_out, projected, gain, mixed, cum):
    half = gated_grad.shape[0] // 2
    per_block, _ = token_specs(half)
    wide = pl.BlockSpec((half, DI), lambda b: (b, 0))
    return pl.pallas_call(
        gated_backward_kernel,
        grid=(2,),
        in_specs=[
            wide,
            wide,
            wide,
            pl.BlockSpec((1, DI), lambda b: (0, 0)),
            pl.BlockSpec((half, NS), lambda b: (b, (DI + NS) // NS)),
            per_block,
        ],
        out_specs=[
            wide,
            wide,
            pl.BlockSpec((1, 1, DI), lambda b: (b, 0, 0)),
            pl.BlockSpec((1, NS, DI), lambda b: (b, 0, 0)),
        ],
        out_shape=[
            jax.ShapeDtypeStruct((2 * half, DI), f32),
            jax.ShapeDtypeStruct((2 * half, DI), bf16),
            jax.ShapeDtypeStruct((2, 1, DI), f32),
            jax.ShapeDtypeStruct((2, NS, DI), bf16),
        ],
        scratch_shapes=[pltpu.VMEM((half, DI), f32), pltpu.VMEM((half, DI), bf16)],
        compiler_params=pltpu.CompilerParams(vmem_limit_bytes=48 * 2**20),
        cost_estimate=pl.CostEstimate(
            flops=4 * half * NS * DI + 60 * half * DI,
            bytes_accessed=40 * half * DI,
            transcendentals=8 * half * DI,
        ),
        name="gated_backward",
    )(gated_grad, scan_out, projected, gain, mixed, cum)


def split_sum(values, spread):
    high, rest = two_halves(values)
    return matmul(high, spread) + matmul(rest, spread)


def scan_backward_kernel(
    m_ref, gy_ref, y_ref, dt_ref, cum_ref, cumt_ref, skip_ref, state_ref, carry_ref,
    dm_ref, dcum_ref, ddt_ref, dskip_ref, last_ref, tail_s, grow_s, blt_s,
):
    half = m_ref.shape[0]
    left = lax.broadcasted_iota(jnp.int32, (half, 2 * MP), 1) < MP
    upper = lax.broadcasted_iota(jnp.int32, (half, half), 0) <= lax.broadcasted_iota(
        jnp.int32, (half, half), 1
    )
    b_rows, b_rest = two_halves(m_ref[:, DI : DI + NS])
    c_rows, c_rest = two_halves(m_ref[:, DI + NS :])
    scores_t = wide_product((b_rows, b_rest), (c_rows, c_rest))
    dt, cum, cum_t = dt_ref[0], cum_ref[0], cumt_ref[0]
    grow = jnp.exp(cum)
    tail = jnp.exp(cum[half - 1 : half, :] - cum)
    fade = grow[half - 1 : half, :]
    carry_low = carry_ref[0]
    blt_s[...] = matmul(b_rows, carry_low)
    d_scores_t = jnp.zeros((half, half), f32)
    d_cum = jnp.zeros((half, 2 * MP), f32)
    d_dt = jnp.zeros((half, 2 * MP), f32)
    lane_head = lax.broadcasted_iota(jnp.int32, (2 * MP, 2 * MP), 0) // MP
    column = lax.broadcasted_iota(jnp.int32, (2 * MP, 2 * MP), 1)
    for pair in range(PAIRS):
        lanes = pair_lanes(pair)
        x, gy = m_ref[:, lanes], gy_ref[:, lanes]
        dt_pair = by_pair(dt, pair, left)
        scaled = x * dt_pair
        gy_low, gy_rest = two_halves(gy)
        scaled_two = two_halves(scaled)
        nothing = jnp.zeros_like(gy_low)
        outs = []
        for k, h in enumerate((2 * pair, 2 * pair + 1)):
            gap = cum_t[h : h + 1, :] - cum[:, h : h + 1]
            decays = jnp.exp(jnp.where(upper, gap, masked_fill_value))
            outs.append(matmul((decays * scores_t).astype(bf16), gy_low))
            mine = [jnp.where(left, v, nothing) if k == 0 else jnp.where(left, nothing, v) for v in scaled_two]
            d_scores_t += wide_product(mine, (gy_low, gy_rest)) * decays
        tail_pair = by_pair(tail, pair, left)
        from_tail = tail_pair * blt_s[:, lanes]
        d_scaled = jnp.where(left, outs[0], outs[1]) + from_tail
        dm_ref[:, lanes] = dt_pair * d_scaled + skip_ref[:, lanes] * gy
        spread = (lane_head + 2 * pair == column).astype(bf16)
        skipped = x * gy
        d_cum += split_sum(gy * y_ref[:, lanes] - skip_ref[:, lanes] * skipped - scaled * d_scaled, spread)
        d_dt += split_sum(x * d_scaled, spread)
        dskip_ref[0, :, lanes] = jnp.sum(skipped, axis=0, keepdims=True)
        held = jnp.sum(state_ref[0][:, lanes].astype(f32) * carry_low[:, lanes].astype(f32), axis=0, keepdims=True)
        last_ref[0, :, lanes] = jnp.sum(scaled * from_tail, axis=0, keepdims=True) + held * by_pair(
            fade, pair, left[0:1]
        )
        tail_s[0, :, lanes], tail_s[1, :, lanes] = two_halves(scaled * tail_pair)
        grow_s[0, :, lanes], grow_s[1, :, lanes] = two_halves(gy * by_pair(grow, pair, left))
    d_low, d_rest = two_halves(d_scores_t)
    dm_ref[:, DI : DI + NS] = (
        matmul(d_low, c_rows)
        + matmul(d_low, c_rest)
        + matmul(d_rest, c_rows)
        + backward_product(tail_s[0], carry_low)
        + backward_product(tail_s[1], carry_low)
    )
    dm_ref[:, DI + NS :] = (
        row_contract(d_low, b_rows)
        + row_contract(d_low, b_rest)
        + row_contract(d_rest, b_rows)
        + backward_product(grow_s[0], state_ref[0])
        + backward_product(grow_s[1], state_ref[0])
    )
    dcum_ref[0] = d_cum[:, :MH]
    ddt_ref[0] = d_dt[:, :MH]


def scan_backward(mixed, scan_grad, scan_out, dt, cum, cum_t, skip_row, states, carries):
    half = mixed.shape[0] // 2
    per_block, per_block_t = token_specs(half)
    wide = pl.BlockSpec((half, DI), lambda b: (b, 0))
    full = pl.BlockSpec((half, CONV), lambda b: (b, 0))
    state = pl.BlockSpec((1, NS, DI), lambda b: (b, 0, 0))
    row = pl.BlockSpec((1, 1, DI), lambda b: (b, 0, 0))
    return pl.pallas_call(
        scan_backward_kernel,
        grid=(2,),
        in_specs=[
            full, wide, wide, per_block, per_block, per_block_t,
            pl.BlockSpec((1, DI), lambda b: (0, 0)), state, state,
        ],
        out_specs=[full, per_block, per_block, row, row],
        out_shape=[
            jax.ShapeDtypeStruct((2 * half, CONV), f32),
            jax.ShapeDtypeStruct((2, half, MH), f32),
            jax.ShapeDtypeStruct((2, half, MH), f32),
            jax.ShapeDtypeStruct((2, 1, DI), f32),
            jax.ShapeDtypeStruct((2, 1, DI), f32),
        ],
        scratch_shapes=[
            pltpu.VMEM((2, half, DI), bf16),
            pltpu.VMEM((2, half, DI), bf16),
            pltpu.VMEM((half, DI), f32),
        ],
        compiler_params=pltpu.CompilerParams(vmem_limit_bytes=56 * 2**20),
        cost_estimate=pl.CostEstimate(
            flops=6 * half * half * 128 * 2 * MH,
            bytes_accessed=40 * half * DI,
            transcendentals=2 * MH * half * half,
        ),
        name="scan_backward",
    )(mixed, scan_grad, scan_out, dt, cum, cum_t, skip_row, states, carries)


def branch_columns(gated, attended):
    shards = lax.axis_size("fsdp")
    one, two = gated.shape[1] // shards, attended.shape[1] // shards
    pieces = []
    for k in range(shards):
        pieces += [gated[:, k * one : (k + 1) * one], attended[:, k * two : (k + 1) * two]]
    return jnp.concatenate(pieces, axis=1)


def branch_split(columns, one, two):
    shards = lax.axis_size("fsdp")
    one, two = one // shards, two // shards
    starts = [k * (one + two) for k in range(shards)]
    return (
        jnp.concatenate([columns[:, k : k + one] for k in starts], axis=1),
        jnp.concatenate([columns[:, k + one : k + one + two] for k in starts], axis=1),
    )


def conv_block(previous, raw_rows, conv_weight, conv_bias):
    extended = jnp.concatenate([previous, raw_rows], axis=0)
    row_count = raw_rows.shape[0]
    running = conv_bias[None, :] + conv_weight[0][None, :] * extended[0:row_count]
    for offset in range(1, conv_weight.shape[0]):
        running = running + conv_weight[offset][None, :] * extended[offset : offset + row_count]
    return jax.nn.silu(running)


def local(
    tokens,
    cotangent,
    block_table,
    mixer_gain,
    in_proj,
    conv_weight,
    conv_bias,
    step_bias,
    decay_log,
    skip_gain,
    gated_gain,
    out_proj,
    attention_in,
    attention_out,
    feed_gain,
    gate_up,
    down_proj,
):
    ctx_count = lax.axis_size("ctx")
    my_index = lax.axis_index("ctx")
    is_last = my_index == ctx_count - 1
    device_rows = tokens.shape[1]
    half_rows = device_rows // 2
    lag_rows = KCONV - 1
    kv_width = KEY_VALUE_HEADS * HEAD_WIDTH
    slot_first = lax.dynamic_index_in_dim(block_table, 2 * my_index, keepdims=False)
    swapped = slot_first != my_index

    def arrange(value_rows):
        first_half = value_rows[:half_rows]
        second_half = value_rows[half_rows:]
        return jnp.concatenate(
            [
                jnp.where(swapped, second_half, first_half),
                jnp.where(swapped, first_half, second_half),
            ],
            axis=0,
        )

    block_ids = jnp.concatenate(
        [
            jnp.full((half_rows,), my_index, jnp.int32),
            jnp.full((half_rows,), 2 * ctx_count - 1 - my_index, jnp.int32),
        ]
    )
    token_positions = block_ids * half_rows + jnp.tile(jnp.arange(half_rows, dtype=jnp.int32), 2)
    freqs = jnp.exp(
        -(jnp.arange(HEAD_WIDTH // 2, dtype=f32) * (2.0 / HEAD_WIDTH)) * jnp.log(rope_base)
    )
    angles = token_positions.astype(f32)[:, None] * freqs[None, :]
    sign = jnp.where(jnp.arange(2 * HEAD_WIDTH) % HEAD_WIDTH < HEAD_WIDTH // 2, -1.0, 1.0)
    cosine, sine = tie(jnp.tile(jnp.cos(angles), (1, 4)), jnp.tile(jnp.sin(angles), (1, 4)) * sign)
    hidden = arrange(tokens[0]).astype(f32)
    out_grad = arrange(cotangent[0]).astype(f32)

    scale_one = norm_scale(hidden)
    normed_one = (hidden * scale_one * mixer_gain).astype(bf16)

    mixer_in, gate_in = in_proj[:, DI:], in_proj[:, :DI]
    branch_rows = jnp.concatenate([out_proj, attention_out], axis=0)
    if lax.axis_size("fsdp") == 4 and ctx_count % 2 == 0:
        qkv_parts = gather_whole(attention_in)
        mixer_in, qkv_parts[2] = tie(mixer_in, qkv_parts[2])
        in_parts = gather_whole(mixer_in)
        full_qkv, full_in = jnp.concatenate(qkv_parts), jnp.concatenate(in_parts)
        order_rows = by_distance
    else:
        full_qkv, full_in = gather_plain(attention_in), gather_plain(mixer_in)
        order_rows = lambda rows: rows
    full_gate_in = gather_plain(gate_in)
    full_branch = gather_plain(branch_rows)
    full_gu = gather_plain(gate_up)
    full_down = gather_plain(down_proj)
    normed_turned = order_rows(normed_one)

    qkv_rows = matmul(normed_turned, full_qkv)
    q_t, pairs = prepare(qkv_rows, cosine, sine)
    outer_pairs = gather_outer(pairs)
    table = pair_table(ctx_count, my_index)
    query_row = jnp.tile(jnp.arange(half_rows, dtype=jnp.int32), GROUP)[None]
    projected = matmul(normed_turned, full_in)
    raw_conv = projected[:, :CONV]
    step_raw = projected[:, CONV:]
    early_tail = raw_conv[half_rows - lag_rows : half_rows]
    edges = jnp.concatenate([raw_conv[device_rows - lag_rows :], early_tail], axis=0)
    before, after = edge_exchange(edges.astype(bf16), lag_rows)
    prev_early = before.astype(f32)
    prev_late = jnp.where(is_last, early_tail, after.astype(f32))
    raw_early = raw_conv[:half_rows]
    raw_late = raw_conv[half_rows:]
    mixed = jnp.concatenate(
        [
            conv_block(prev_early, raw_early, conv_weight, conv_bias),
            conv_block(prev_late, raw_late, conv_weight, conv_bias),
        ],
        axis=0,
    )
    mixed, *outer_pairs = tie(mixed, *outer_pairs)
    outer_pairs = jnp.stack(outer_pairs)
    inner_pairs = swap(outer_pairs, "ctx", 1)
    step_size = jax.nn.softplus(step_raw + step_bias[None, :])
    decay_rate = -jnp.exp(decay_log)
    dt = step_size.reshape(2, half_rows, MH)
    lower = jnp.tril(jnp.ones((half_rows, half_rows), f32))
    cum = jnp.einsum("ts,bsh->bth", lower, dt * decay_rate, precision=highest)
    cum_t = cum.swapaxes(1, 2)
    skip_row = jnp.repeat(skip_gain, MP)[None]
    fades = jnp.broadcast_to(jnp.exp(cum[:, half_rows - 1]), (ctx_count, 2, MH))
    fades = lax.all_to_all(fades, "ctx", 0, 0)
    fades = jnp.repeat(fades.reshape(2 * ctx_count, MH), MP, axis=1)
    part, updates = scan_forward(mixed, dt, cum, cum_t, skip_row)

    block = jnp.arange(2 * ctx_count, dtype=jnp.int32)
    block_late = block >= ctx_count
    block_device = jnp.where(block_late, 2 * ctx_count - 1 - block, block)
    order = block_device * 2 + block_late.astype(jnp.int32)
    updates, inner_pairs = tie(updates, inner_pairs)
    all_pairs = jnp.stack([outer_pairs, inner_pairs], axis=1)
    all_pairs = all_pairs.reshape(2 * ctx_count, half_rows, 2 * kv_width)
    pieces = send_updates(updates)
    gate_z, pieces = tie(matmul(normed_one, full_gate_in), pieces)
    states = return_states(run_states(order, pieces, fades))
    attn_low, attn_t, log_total = attn_forward(table, q_t, all_pairs, query_row)
    states, attn_low = tie(states, attn_low)
    gain_row = gated_gain[None]
    scan_out, gated_low = gated_forward(part, mixed, cum, states, gate_z, gain_row)

    second = hidden + matmul(branch_columns(gated_low, attn_low), full_branch)
    scale_two = norm_scale(second)
    normed_two = (second * scale_two * feed_gain).astype(bf16)
    gate_rows = matmul(normed_two, full_gu)
    gate_part = gate_rows[:, :FF]
    up_part = gate_rows[:, FF:]
    sig_gate = jax.nn.sigmoid(gate_part)
    silu_gate = gate_part * sig_gate
    activated = (silu_gate * up_part).astype(bf16)
    result = second + matmul(activated, full_down)

    down_grad = out_grad.astype(bf16)
    d_model = hidden.shape[1]
    down_part = rows_by_owner(row_contract(activated, down_grad))
    act_grad = backward_product(down_grad, full_down)
    gate_grad = act_grad * up_part * sig_gate * (1.0 + gate_part * (1.0 - sig_gate))
    up_grad = act_grad * silu_gate
    gu_grad = jnp.concatenate([gate_grad, up_grad], axis=1).astype(bf16)
    gu_parts = [
        rows_by_owner(row_contract(normed_two, gu_grad[:, k : k + d_model])) for k in range(0, 2 * FF, d_model)
    ]
    normed_two_grad = backward_product(gu_grad, full_gu)
    grad_feed = jnp.sum(normed_two_grad * second * scale_two, axis=0)
    resid_grad = out_grad + norm_backward(normed_two_grad * feed_gain, second, scale_two)
    branch_gradient = resid_grad.astype(bf16)
    gated_grad, attn_grad = branch_split(
        backward_product(branch_gradient, full_branch), DI, QUERY_HEADS * HEAD_WIDTH
    )
    scan_grad, z_grad, gain_parts, direct = gated_backward(
        gated_grad, scan_out, gate_z, gain_row, mixed, cum
    )
    grad_gated = jnp.sum(gain_parts[:, 0], axis=0)
    pieces = send_updates(direct)

    attn_grad, pieces = tie(attn_grad.astype(bf16), pieces)
    carries = return_states(run_states(order[::-1], pieces, fades))
    z_part = rows_by_owner(row_contract(normed_one, z_grad[:, :d_model]))
    z_rest = rows_by_owner(row_contract(normed_one, z_grad[:, d_model:]))
    z_half = z_rest.shape[4] // 2
    views = [
        rows_by_owner(row_contract(gated_low, branch_gradient)),
        rows_by_owner(row_contract(attn_low, branch_gradient)),
        z_part,
        jnp.concatenate([z_rest[..., :z_half, :], z_rest[..., z_half:, :]], axis=5),
    ]
    views = gu_parts + [down_part] + views
    attn_grad, flat = tie(attn_grad, jnp.concatenate(views, axis=4))
    sums = sum_all(flat)
    dq, d_pairs = attn_backward(
        table, q_t, all_pairs, attn_grad, attn_t, log_total, cosine, sine, query_row
    )
    d_pairs, carries = tie(d_pairs, carries)
    d_pairs = d_pairs.reshape(ctx_count // 2, 2, device_rows, 2 * kv_width)
    pairs_sent, scan_grad = tie(d_pairs[:, 1], scan_grad)
    pairs_came = swap(pairs_sent, "ctx", 1)
    mixed_grad, d_cum, d_dt, skip_parts, last_parts = scan_backward(
        mixed, scan_grad, scan_out, dt, cum, cum_t, skip_row, states, carries
    )
    grad_skip = jnp.sum(skip_parts.reshape(2, MH, MP), axis=(0, 2))
    last = jnp.sum(last_parts.reshape(2, MH, MP), axis=2)
    log_grad = jnp.einsum("ts,bth->bsh", lower, d_cum, precision=highest) + last[:, None, :]
    grad_decay = jnp.sum(log_grad * dt, axis=(0, 1)) * decay_rate
    step_grad = (d_dt + log_grad * decay_rate).reshape(device_rows, MH)
    step_raw_grad = step_grad * jax.nn.sigmoid(step_raw + step_bias[None, :])
    grad_step = jnp.sum(step_raw_grad, axis=0)
    _, conv_pull_early = jax.vjp(conv_block, prev_early, raw_early, conv_weight, conv_bias)
    prev_early_grad, raw_early_grad, weight_early_grad, bias_early_grad = conv_pull_early(
        mixed_grad[:half_rows]
    )
    _, conv_pull_late = jax.vjp(conv_block, prev_late, raw_late, conv_weight, conv_bias)
    prev_late_grad, raw_late_grad, weight_late_grad, bias_late_grad = conv_pull_late(
        mixed_grad[half_rows:]
    )
    backs = jnp.concatenate([prev_early_grad, prev_late_grad], axis=0)
    before_g, after_g = edge_exchange(backs.astype(bf16), lag_rows)
    before_g, after_g, pairs_came = tie(before_g, after_g, pairs_came)
    early_tail_grad = after_g.astype(f32) + jnp.where(is_last, prev_late_grad, 0.0)
    late_tail_grad = before_g.astype(f32)
    raw_early_grad = raw_early_grad.at[half_rows - lag_rows :].add(early_tail_grad)
    raw_late_grad = raw_late_grad.at[half_rows - lag_rows :].add(late_tail_grad)
    raw_grad = jnp.concatenate([raw_early_grad, raw_late_grad], axis=0)
    wide_grad = jnp.concatenate([raw_grad.astype(bf16), step_raw_grad.astype(bf16)], axis=1)
    tail_width = CONV + MH
    padded_grad = jnp.pad(wide_grad, ((0, 0), (0, -tail_width % 128)))

    kept, came = send_core(rows_by_owner(row_contract(normed_one, padded_grad)))
    own_pairs = (d_pairs[:, 0].astype(f32) + pairs_came.astype(f32)).astype(bf16)
    pair_terms = [own_pairs[0]] + [swap(own_pairs[k // 2], "ctx", k) for k in range(2, ctx_count, 2)]
    wide_terms = first_terms([kept, came])
    count = len(pair_terms)
    tied = tie(*pair_terms, *wide_terms)
    pair_terms, wide_terms = tied[:count], tied[count:]
    pair_grad = add_up(pair_terms)
    key_grad = pair_grad[:, :kv_width]
    quarter = HEAD_WIDTH // 2
    key_swapped = jnp.concatenate(
        [key_grad[:, k * quarter : (k + 1) * quarter] for k in (1, 0, 3, 2)], axis=1
    )
    qkv_grad = jnp.concatenate(
        [dq, (key_grad * cosine - key_swapped * sine).astype(bf16), pair_grad[:, kv_width:].astype(bf16)],
        axis=1,
    )
    kept, came = send_core(rows_by_owner(row_contract(normed_one, qkv_grad)))
    wide_terms = second_terms(wide_terms)
    came, *wide_terms = tie(came, *wide_terms)
    normed_one_grad = order_rows(
        backward_product(qkv_grad, full_qkv) + backward_product(wide_grad, full_in)
    ) + backward_product(z_grad, full_gate_in)
    grad_mixer = jnp.sum(normed_one_grad * hidden * scale_one, axis=0)
    input_grad = resid_grad + norm_backward(normed_one_grad * mixer_gain, hidden, scale_one)

    small = (
        grad_mixer,
        grad_gated,
        grad_feed,
        (weight_early_grad + weight_late_grad).reshape(-1),
        bias_early_grad + bias_late_grad,
        grad_step,
        grad_decay,
        grad_skip,
    )
    flat = jnp.concatenate(small)
    size = flat.shape[0]
    flat = jnp.pad(flat, (0, -size % 1024)).reshape(-1, 128)
    wide_terms, qkv_terms = last_terms(wide_terms), first_terms([kept, came])
    count = len(wide_terms)
    flat, *tied = tie(all_sum(flat, "fsdp", 1, lax.axis_size("fsdp")), *wide_terms, *qkv_terms)
    grad_wide, qkv_terms = add_up(tied[:count]), second_terms(tied[count:])
    flat, *qkv_terms = tie(all_sum(flat, "ctx", 1, 2), *qkv_terms)
    grad_qkv = add_up(last_terms(qkv_terms))
    flat = all_sum(flat, "ctx", 2, ctx_count).reshape(-1)
    pieces, start = [], 0
    for view in views:
        pieces.append(sums[start : start + view.shape[4]])
        start += view.shape[4]
    grad_gu = jnp.concatenate(pieces[: len(gu_parts)], axis=1)
    grad_down, grad_out, grad_o, grad_z, z_rest = pieces[len(gu_parts) :]
    z_rest = jnp.concatenate([z_rest[:, : d_model // 2], z_rest[:, d_model // 2 :]], axis=0)
    grad_in = jnp.concatenate([grad_z, z_rest, grad_wide[:, :tail_width]], axis=1)
    sums, start = [], 0
    for piece in small:
        sums.append(flat[start : start + piece.shape[0]])
        start += piece.shape[0]
    return (
        arrange(result).astype(bf16)[None],
        arrange(input_grad)[None],
        sums[0],
        grad_in,
        sums[3].reshape(conv_weight.shape),
        sums[4],
        sums[5],
        sums[6],
        sums[7],
        sums[1],
        grad_out,
        grad_qkv,
        grad_o,
        sums[2],
        grad_gu,
        grad_down,
    )


def solution(mesh):
    rows = P("fsdp", None)
    spread = P(("ctx", "fsdp"), None)
    tokens = P("fsdp", "ctx", None)
    return jax.shard_map(
        local,
        mesh=mesh,
        in_specs=(
            tokens, tokens, P(), P(), rows, P(), P(), P(), P(), P(), P(), rows, rows, rows, P(), rows, rows,
        ),
        out_specs=(
            tokens, tokens, P(), spread, P(), P(), P(), P(), P(), P(), spread, spread, spread, P(), spread, spread,
        ),
        check_vma=False,
    )
```
